32 devices in a mesh: grp: 2 (over y), row: 4 (over z), col: 4 (over x, core).
Axes of the slice: x: 2, y: 2, z: 4, core: 2. Of those that a mesh axis runs over, the one named last changes fastest.
Arguments:
- matrix: bfloat16 [8192, 16384], P(('grp', 'row'), 'col'), parts along dimension 0, may hold values from -6 to 6
- row_factor: float32 [8192, 128], P(('grp', 'row')), parts along dimension 0, may hold values from -1.8 to 1.8
- col_factor: float32 [32768, 128], P(('grp', 'col')), parts along dimension 0, may hold values from -1.8 to 1.8
- row_mean: float32 [8192, 128], P(('grp', 'row')), parts along dimension 0
- row_square: float32 [8192, 128], P(('grp', 'row')), parts along dimension 0, may hold values from 6.1035155e-07 to 1.2207031e-05
- col_mean: float32 [32768, 128], P(('grp', 'col')), parts along dimension 0
- col_square: float32 [32768, 128], P(('grp', 'col')), parts along dimension 0, may hold values from 2.4414064e-07 to 2.4414062e-06
Outputs:
- new_rows: float32 [8192, 128], P(('grp', 'row')), parts along dimension 0
- new_cols: float32 [32768, 128], P(('grp', 'col')), parts along dimension 0
The draws below stay inside these ranges and needn't reach their ends.
There are 2 independent parts, one for each index of `grp`. The reference program is written for one: setup_inputs(seed, part) draws one part's arguments, and reference() takes and returns one part's arrays. A program takes and returns all parts, laid end to end along the dimension named above; each array names one. Nothing has to cross between parts.
All inputs are finite; a program needn't handle non-finite values.
Results may differ from the reference program's by a relative error of at most 0.0003.
Values sent between devices are 32-bit elements; how exact they have to be, the bound alone decides.
No kernel may reach another device: no remote copies, remote signals or barrier semaphores. Data moves between devices by JAX's collectives and lax.ppermute only.
A program may use at most 128 MiB of HBM per device.

```python
import math
import jax
import jax.numpy as jnp
from jax import lax

K = 128
START = 100
R = 4096
C = 16384
N_ROW = 4


def moment_draw(key, rows, spread):
    values = jax.random.normal(key, (rows, K), jnp.float32)
    return values * spread


def draw_row_mean(key, part):
    key = jax.random.fold_in(key, 11)
    return moment_draw(key, R, 0.2 / math.sqrt(C))


def draw_col_mean(key, part):
    key = jax.random.fold_in(key, 23)
    return moment_draw(key, C, 0.2 / math.sqrt(R))


def shard_levels(rng, shape, split, least, top_value):
    loudness = 1.0
    for axis_at, shards_of in split:
        draws = jax.random.uniform(jax.random.fold_in(jax.random.fold_in(rng, 6), axis_at), (shards_of,), jnp.float32, least / len(split), top_value / len(split))
        loudness = loudness * jnp.repeat(jnp.exp(draws), shape[axis_at] // shards_of).reshape((-1,) + (1,) * (len(shape) - 1 - axis_at))
    return loudness


def centred(rng, dims, scale, limit, cuts=(), kind=jnp.bfloat16):
    loudness = shard_levels(rng, dims, cuts, -0.22, 0.18) if cuts else 1.0
    values = jax.random.normal(rng, dims, jnp.float32) * scale * loudness
    return jnp.minimum(jnp.maximum(values, -limit), limit).astype(kind)


def setup_inputs(seed: int = 0, part: int = 0) -> dict:
    seeds = jax.random.split(jax.random.key(seed), 8)
    part_keys = jax.random.split(jax.random.fold_in(seeds[7], part), 8)
    return {
        "matrix": centred(part_keys[0], (R, C), 1.0, 6.0, ((0, 4), (1, 4))),
        "row_factor": centred(part_keys[1], (R, K), 0.3, 1.8, ((0, 4),), jnp.float32),
        "col_factor": centred(part_keys[2], (C, K), 0.3, 1.8, ((0, 4),), jnp.float32),
        "row_mean": draw_row_mean(jax.random.fold_in(jax.random.fold_in(seeds[7], part), 71), part),
        "row_square": jnp.clip(jnp.exp(math.log(1.220703143189894e-05) - 2.9957323 * jax.random.uniform(part_keys[4], (R, K), jnp.float32) ** shard_levels(part_keys[4], (R, K), ((0, 4),), -0.2, 0.2)), 6.103515488575795e-07, 1.220703143189894e-05),
        "col_mean": draw_col_mean(jax.random.fold_in(jax.random.fold_in(seeds[7], part), 71), part),
        "col_square": jnp.clip(jnp.exp(math.log(2.441406195430318e-06) - 2.30258502 * jax.random.uniform(part_keys[6], (C, K), jnp.float32) ** shard_levels(part_keys[6], (C, K), ((0, 4),), -0.2, 0.2)), 2.4414063659605745e-07, 2.441406195430318e-06),
    }


DELTA = 1.0
LEARN_RATE = 0.05
BETA_ONE = 0.9
BETA_TWO = 0.999
EPSILON = 1e-08
HIGH = lax.Precision.HIGHEST

def adam_move(values, gradient, first_moment, square, counter):
    first_moment = BETA_ONE * first_moment + (1.0 - BETA_ONE) * gradient
    square = BETA_TWO * square + (1.0 - BETA_TWO) * gradient * gradient
    fixed_mean = first_moment / (1.0 - BETA_ONE ** counter)
    fixed_square = square / (1.0 - BETA_TWO ** counter)
    return (values - LEARN_RATE * fixed_mean / (jnp.sqrt(fixed_square) + EPSILON), first_moment, square)

def clipped(block, row_part, col_part):
    fitted = lax.dot_general(row_part, col_part, (((1,), (1,)), ((), ())), precision=HIGH)
    return jnp.clip(fitted - block.astype(jnp.float32), -DELTA, DELTA)

def col_gradient(matrix, row_factor, col_factor):
    blocks = matrix.reshape(N_ROW, R // N_ROW, C)
    row_blocks = row_factor.reshape(N_ROW, R // N_ROW, K)

    def accumulate(summed, pieces):
        block, row_part = pieces
        slopes = clipped(block, row_part, col_factor)
        return (summed + lax.dot_general(slopes, row_part, (((0,), (0,)), ((), ())), precision=HIGH), None)
    summed, _ = lax.scan(accumulate, jnp.zeros((C, K), jnp.float32), (blocks, row_blocks))
    return summed

def row_gradient(matrix, row_factor, col_factor):
    blocks = matrix.reshape(N_ROW, R // N_ROW, C)
    row_blocks = row_factor.reshape(N_ROW, R // N_ROW, K)

    def one_block(pieces):
        block, row_part = pieces
        return jnp.dot(clipped(block, row_part, col_factor), col_factor, precision=HIGH)
    return lax.map(one_block, (blocks, row_blocks)).reshape(R, K)

def reference(matrix, row_factor, col_factor, row_mean, row_square, col_mean, col_square):
    for inner_step in range(2):
        gradient = col_gradient(matrix, row_factor, col_factor) / R
        col_factor, col_mean, col_square = adam_move(col_factor, gradient, col_mean, col_square, START + 1 + inner_step)
    gradient = row_gradient(matrix, row_factor, col_factor) / C
    new_rows, unused_mean, unused_square = adam_move(row_factor, gradient, row_mean, row_square, START + 1)
    return (new_rows, col_factor)
```

```python
import functools

import jax
import jax.numpy as jnp
from jax import lax
from jax.experimental import pallas as pl
from jax.experimental.pallas import tpu as pltpu
from jax.sharding import PartitionSpec as P

START = 100
DELTA = 1.0
LEARN_RATE = 0.05
BETA_ONE = 0.9
BETA_TWO = 0.999
EPSILON = 1e-08
F32, BF16 = jnp.float32, jnp.bfloat16
NT = (((1,), (1,)), ((), ()))
ROW_BLOCK = 256
CHUNKS = 8
LAG = 2


def adam_move(values, gradient, first_moment, square, counter):
    first_moment = BETA_ONE * first_moment + (1.0 - BETA_ONE) * gradient
    square = BETA_TWO * square + (1.0 - BETA_TWO) * gradient * gradient
    fixed_mean = first_moment / (1.0 - BETA_ONE**counter)
    fixed_square = square / (1.0 - BETA_TWO**counter)
    return (
        values - LEARN_RATE * fixed_mean / (jnp.sqrt(fixed_square) + EPSILON),
        first_moment,
        square,
    )


def split(values):
    high = values.astype(BF16)
    return high, (values - high.astype(F32)).astype(BF16)


def slopes_of(row_pair, col_pair, block):
    fitted = lax.dot_general(row_pair, col_pair, NT, preferred_element_type=F32)
    return jnp.clip(fitted - block.astype(F32), -DELTA, DELTA).astype(BF16)


def col_partial(twice_ref, turned_ref, col, mat_ref, first_col):
    col_pair = jnp.concatenate(split(col), axis=1)
    width, rank = col.shape
    total = None
    for at in range(0, mat_ref.shape[0], ROW_BLOCK):
        rows = pl.ds(at, ROW_BLOCK)
        slopes = slopes_of(twice_ref[rows, :], col_pair, mat_ref[rows, pl.ds(first_col, width)])
        term = jnp.dot(turned_ref[:, rows], slopes, preferred_element_type=F32)
        total = term if total is None else total + term
    return (total[:rank] + total[rank:]).T


def first_kernel(row_ref, col_ref, mat_ref, twice_ref, pair_ref, turned_ref, out_ref):
    high, low = split(row_ref[...])
    twice_ref[...] = jnp.concatenate([high, high], axis=1)
    pair_ref[...] = jnp.concatenate([high, low], axis=1)
    turned_ref[...] = jnp.concatenate([high.T, low.T], axis=0)
    out_ref[...] = col_partial(twice_ref, turned_ref, col_ref[...], mat_ref, 0)


def fresh_kernel(at, token_ref, twice_ref, turned_ref, col_ref, mat_ref, out_ref):
    del token_ref
    width = out_ref.shape[0]
    col = col_ref[pl.ds(at, width), :]
    out_ref[...] = col_partial(twice_ref, turned_ref, col, mat_ref, at)


def middle_kernel(
    at, rows_total, token_ref, twice_ref, turned_ref, sum_ref, col_ref, mean_ref, square_ref, mat_ref,
    new_ref, new_mean_ref, new_square_ref, out_ref,
):
    del token_ref
    own = pl.ds(at, out_ref.shape[0])
    new, new_mean_ref[...], new_square_ref[...] = adam_move(
        col_ref[own, :], sum_ref[...] / rows_total, mean_ref[own, :], square_ref[own, :], START + 1
    )
    new_ref[...] = new
    out_ref[...] = col_partial(twice_ref, turned_ref, new, mat_ref, at)


def last_kernel(
    at, rows_total, token_ref, pair_ref, sum_ref, col_ref, mean_ref, square_ref, mat_ref, grad_ref,
    new_ref, out_ref,
):
    del token_ref
    new, _, _ = adam_move(
        col_ref[...], sum_ref[...] / rows_total, mean_ref[...], square_ref[...], START + 2
    )
    new_ref[...] = new
    high, low = split(new)
    twice = jnp.concatenate([high, high], axis=1)
    pair = jnp.concatenate([high, low], axis=1)
    width, rank = new.shape
    for at_row in range(0, mat_ref.shape[0], ROW_BLOCK):
        rows = pl.ds(at_row, ROW_BLOCK)
        slopes = slopes_of(pair_ref[rows, :], twice, mat_ref[rows, pl.ds(at, width)])
        term = jnp.dot(slopes, pair, preferred_element_type=F32)
        out_ref[rows, :] = grad_ref[rows, :] + term[:, :rank] + term[:, rank:]


def call(kernel, outs, *args, name, token=None):
    vmem = pl.BlockSpec(memory_space=pltpu.VMEM)
    in_specs = [vmem] * len(args)
    if token is not None:
        in_specs, args = [pl.BlockSpec(memory_space=pl.ANY), *in_specs], (token, *args)
    return pl.pallas_call(
        kernel,
        out_shape=[jax.ShapeDtypeStruct(shape, kind) for shape, kind in outs],
        in_specs=in_specs,
        out_specs=[vmem] * len(outs),
        compiler_params=pltpu.CompilerParams(vmem_limit_bytes=16 << 20),
        name=name,
    )(*args)


class Work:
    def __init__(self, matrix, row_factor, col_factor, col_mean, col_square, rows_total):
        self.matrix, self.row, self.rows_total = matrix, row_factor, rows_total
        self.col, self.mean, self.square = col_factor, col_mean, col_square
        self.width = col_factor.shape[0] // CHUNKS
        self.rank = col_factor.shape[1]
        self.small = ((self.width, self.rank), F32)
        self.moved = {}
        self.new = {}
        self.grad = jnp.zeros(row_factor.shape, F32)

    def first(self):
        rows, rank = self.row.shape
        wide = ((rows, 2 * rank), BF16)
        self.twice, self.pair, self.turned, out = call(
            first_kernel,
            [wide, wide, ((2 * rank, rows), BF16), self.small],
            self.row, self.col[: self.width], self.matrix[:, : self.width],
            name="first",
        )
        return out

    def fresh(self, chunk, token):
        (out,) = call(
            functools.partial(fresh_kernel, chunk * self.width),
            [self.small],
            self.twice, self.turned, self.col, self.matrix,
            name="fresh", token=token,
        )
        return out

    def middle(self, chunk, total, token):
        *self.moved[chunk], out = call(
            functools.partial(middle_kernel, chunk * self.width, self.rows_total),
            [self.small] * 4,
            self.twice, self.turned, total, self.col, self.mean, self.square, self.matrix,
            name="middle", token=token,
        )
        return out

    def last(self, chunk, total, token):
        self.new[chunk], self.grad = call(
            functools.partial(last_kernel, chunk * self.width, self.rows_total),
            [self.small, (self.row.shape, F32)],
            self.pair, total, *self.moved[chunk], self.matrix, self.grad,
            name="last", token=token,
        )


def plain_columns(work):
    sums = [lax.psum(work.first(), "row")]
    for chunk in range(1, CHUNKS):
        sums.append(lax.psum(work.fresh(chunk, sums[0]), "row"))
    sums = [lax.psum(work.middle(chunk, sums[chunk], sums[chunk]), "row") for chunk in range(CHUNKS)]
    for chunk in range(CHUNKS):
        work.last(chunk, sums[chunk], sums[chunk])


def line_columns(work):
    n_col = lax.axis_size("col")
    row = lax.axis_index("row")
    outer = (row == 0) | (row == 3)
    outer_pairs = [(0, 1), (1, 0), (2, 3), (3, 2)]
    inner_pairs = []
    for col in range(n_col):
        inner_pairs += [(n_col + col, 2 * n_col + col), (2 * n_col + col, n_col + col)]
        inner_pairs += [(at * n_col + col, at * n_col + (col ^ 1)) for at in (0, 3)]
    slots = 2 * CHUNKS
    own, joined, whole, from_outer, from_inner = {}, {}, {}, {}, {}
    own[0] = work.first()
    token = own[0]
    for k in range(slots + 4 * LAG):
        if 0 <= k - LAG < slots:
            joined[k - LAG] = own[k - LAG] + from_outer[k - LAG]
        if 0 <= k - 2 * LAG < slots:
            whole[k - 2 * LAG] = joined[k - 2 * LAG] + from_inner[k - LAG]
        if k < slots + 2 * LAG:
            if k < 2 * LAG:
                payload = own[k]
            elif k < slots:
                payload = jnp.where(outer, own[k], whole[k - 2 * LAG])
            else:
                payload = whole[k - 2 * LAG]
            token = payload
            from_outer[k] = lax.ppermute(payload, "row", outer_pairs)
        if 0 <= k - LAG < slots:
            from_inner[k] = lax.ppermute(joined[k - LAG], ("row", "col"), inner_pairs)
        nxt = k + 1
        if nxt < CHUNKS:
            own[nxt] = work.fresh(nxt, token)
        elif nxt < slots:
            done = nxt - CHUNKS
            total = jnp.where(outer, from_outer[done + 2 * LAG], whole[done])
            own[nxt] = work.middle(done, total, token)
        done = k - 3 * LAG
        if CHUNKS <= done < slots:
            total = jnp.where(outer, from_outer[done + 2 * LAG], whole[done])
            work.last(done - CHUNKS, total, token)


def row_step(grad, row_factor, row_mean, row_square, cols_total):
    half = grad.shape[0] // 2
    high = lax.rem(lax.axis_index("col"), 2) == 1
    swap = [(0, 1), (1, 0), (2, 3), (3, 2)]
    across = [(0, 2), (2, 0), (1, 3), (3, 1)]

    def mine(array):
        return jnp.where(high, array[half:], array[:half])

    part = mine(grad) + lax.ppermute(jnp.where(high, grad[:half], grad[half:]), "col", swap)
    part = part + lax.ppermute(part, "col", across)
    new, _, _ = adam_move(
        mine(row_factor), part / cols_total, mine(row_mean), mine(row_square), START + 1
    )
    other = lax.ppermute(new, "col", swap)
    return jnp.concatenate([jnp.where(high, other, new), jnp.where(high, new, other)], axis=0)


def on_device(matrix, row_factor, col_factor, row_mean, row_square, col_mean, col_square):
    n_row = lax.axis_size("row")
    n_col = lax.axis_size("col")
    work = Work(matrix, row_factor, col_factor, col_mean, col_square, matrix.shape[0] * n_row)
    if n_row == 4 and n_col % 2 == 0:
        line_columns(work)
    else:
        plain_columns(work)
    cols_total = matrix.shape[1] * n_col
    if n_col == 4:
        new_rows = row_step(work.grad, row_factor, row_mean, row_square, cols_total)
    else:
        summed = lax.psum(work.grad, "col")
        new_rows, _, _ = adam_move(row_factor, summed / cols_total, row_mean, row_square, START + 1)
    return new_rows, jnp.concatenate([work.new[chunk] for chunk in range(CHUNKS)], axis=0)


def solution(mesh):
    return jax.shard_map(
        on_device,
        mesh=mesh,
        in_specs=(
            P(("grp", "row"), "col"),
            P(("grp", "row"), None),
            P(("grp", "col"), None),
            P(("grp", "row"), None),
            P(("grp", "row"), None),
            P(("grp", "col"), None),
            P(("grp", "col"), None),
        ),
        out_specs=(P(("grp", "row"), None), P(("grp", "col"), None)),
        check_vma=False,
    )
```

```python
import functools

import jax
import jax.numpy as jnp
from jax import lax
from jax.experimental import pallas as pl
from jax.experimental.pallas import tpu as pltpu
from jax.sharding import PartitionSpec as P

START = 100
DELTA = 1.0
LEARN_RATE = 0.05
BETA_ONE = 0.9
BETA_TWO = 0.999
EPSILON = 1e-08
F32, BF16 = jnp.float32, jnp.bfloat16
NT = (((1,), (1,)), ((), ()))
ROW_BLOCK = 256
UNIT = 128
TARGET = 384
LAG = 2


def adam_move(values, gradient, first_moment, square, counter):
    first_moment = BETA_ONE * first_moment + (1.0 - BETA_ONE) * gradient
    square = BETA_TWO * square + (1.0 - BETA_TWO) * gradient * gradient
    fixed_mean = first_moment / (1.0 - BETA_ONE**counter)
    fixed_square = square / (1.0 - BETA_TWO**counter)
    return (
        values - LEARN_RATE * fixed_mean / (jnp.sqrt(fixed_square) + EPSILON),
        first_moment,
        square,
    )


def split(values):
    high = values.astype(BF16)
    return high, (values - high.astype(F32)).astype(BF16)


def slopes_of(row_pair, col_pair, block):
    fitted = lax.dot_general(row_pair, col_pair, NT, preferred_element_type=F32)
    return jnp.clip(fitted - block.astype(F32), -DELTA, DELTA).astype(BF16)


def col_partial(twice_ref, turned_ref, col, mat_ref, first_col):
    col_pair = jnp.concatenate(split(col), axis=1)
    width, rank = col.shape
    total = None
    for at in range(0, mat_ref.shape[0], ROW_BLOCK):
        rows = pl.ds(at, ROW_BLOCK)
        slopes = slopes_of(twice_ref[rows, :], col_pair, mat_ref[rows, pl.ds(first_col, width)])
        term = jnp.dot(turned_ref[:, rows], slopes, preferred_element_type=F32)
        total = term if total is None else total + term
    return (total[:rank] + total[rank:]).T


def first_kernel(outer_ref, high_ref, row_ref, col_ref, mat_ref, twice_ref, pair_ref, turned_ref, out_ref):
    del outer_ref, high_ref
    high, low = split(row_ref[...])
    twice_ref[...] = jnp.concatenate([high, high], axis=1)
    pair_ref[...] = jnp.concatenate([high, low], axis=1)
    turned_ref[...] = jnp.concatenate([high.T, low.T], axis=0)
    out_ref[...] = col_partial(twice_ref, turned_ref, col_ref[: out_ref.shape[0], :], mat_ref, 0)


def pick(outer_ref, far_ref, near_ref):
    near = near_ref[...]
    return jnp.where(outer_ref[0] == 1, far_ref[: near.shape[0], :], near)


def fresh_kernel(at, token_ref, twice_ref, turned_ref, col_ref, mat_ref, out_ref):
    del token_ref
    width = out_ref.shape[0]
    col = col_ref[pl.ds(at, width), :]
    out_ref[...] = col_partial(twice_ref, turned_ref, col, mat_ref, at)


def middle_kernel(
    at, rows_total, token_ref, outer_ref, far_ref, near_ref, twice_ref, turned_ref, mat_ref, col_ref, mean_ref,
    square_ref, new_ref, new_mean_ref, new_square_ref, out_ref,
):
    del token_ref
    total = pick(outer_ref, far_ref, near_ref)
    own = pl.ds(at, out_ref.shape[0])
    new, new_mean_ref[...], new_square_ref[...] = adam_move(
        col_ref[own, :], total / rows_total, mean_ref[own, :], square_ref[own, :], START + 1
    )
    new_ref[...] = new
    out_ref[...] = col_partial(twice_ref, turned_ref, new, mat_ref, at)


def last_kernel(at, rows_total, begun, *refs):
    _, outer_ref, far_ref, near_ref, pair_ref, mat_ref, col_ref, mean_ref, square_ref, *grad_ref = refs[:-2]
    new_ref, out_ref = refs[-2:]
    total = pick(outer_ref, far_ref, near_ref)
    width, rank = total.shape
    own = pl.ds(at, width)
    new, _, _ = adam_move(
        col_ref[...], total / rows_total, mean_ref[...], square_ref[...], START + 2
    )
    new_ref[...] = new
    high, low = split(new)
    twice = jnp.concatenate([high, high], axis=1)
    pair = jnp.concatenate([high, low], axis=1)
    for at_row in range(0, mat_ref.shape[0], ROW_BLOCK):
        rows = pl.ds(at_row, ROW_BLOCK)
        slopes = slopes_of(pair_ref[rows, :], twice, mat_ref[rows, own])
        term = jnp.dot(slopes, pair, preferred_element_type=F32)
        term = term[:, :rank] + term[:, rank:]
        out_ref[rows, :] = grad_ref[0][rows, :] + term if begun else term


def store_kernel(token_ref, *refs):
    del token_ref
    *chunk_refs, out_hbm, done_ref, sems = refs
    done_ref[...] = jnp.zeros_like(done_ref)
    stores, at = [], 0
    for index, chunk_ref in enumerate(chunk_refs):
        target = out_hbm.at[pl.ds(at, chunk_ref.shape[0]), :]
        stores.append(pltpu.make_async_copy(chunk_ref, target, sems.at[index]))
        at += chunk_ref.shape[0]
    for store in stores:
        store.start()
    for store in stores:
        store.wait()


def halves_kernel(high_ref, grad_ref, keep_ref, send_ref):
    half = keep_ref.shape[0]
    keep_ref[...] = grad_ref[pl.ds(pl.multiple_of(high_ref[0] * half, half), half), :]
    send_ref[...] = grad_ref[pl.ds(pl.multiple_of((1 - high_ref[0]) * half, half), half), :]


def row_kernel(cols_total, token_ref, high_ref, part_ref, other_ref, row_ref, mean_ref, square_ref, new_ref):
    del token_ref
    half = part_ref.shape[0]
    own = pl.ds(pl.multiple_of(high_ref[0] * half, half), half)
    gradient = (part_ref[...] + other_ref[...]) / cols_total
    new_ref[...], _, _ = adam_move(row_ref[own, :], gradient, mean_ref[own, :], square_ref[own, :], START + 1)


def join_kernel(high_ref, new_ref, other_ref, out_hbm, sems):
    half = new_ref.shape[0]
    own = pl.multiple_of(high_ref[0] * half, half)
    far = pl.multiple_of((1 - high_ref[0]) * half, half)
    stores = [
        pltpu.make_async_copy(new_ref, out_hbm.at[pl.ds(own, half), :], sems.at[0]),
        pltpu.make_async_copy(other_ref, out_hbm.at[pl.ds(far, half), :], sems.at[1]),
    ]
    for store in stores:
        store.start()
    for store in stores:
        store.wait()


VMEM = pl.BlockSpec(memory_space=pltpu.VMEM)
SMEM = pl.BlockSpec(memory_space=pltpu.SMEM)
ANY = pl.BlockSpec(memory_space=pl.ANY)
HBM = pl.BlockSpec(memory_space=pltpu.HBM)


def call(kernel, name, ins, outs, scratch=(), aliases=None):
    return pl.pallas_call(
        kernel,
        out_shape=[jax.ShapeDtypeStruct(shape, kind) for _, shape, kind in outs],
        in_specs=[spec for spec, _ in ins],
        out_specs=[spec for spec, _, _ in outs],
        scratch_shapes=scratch,
        input_output_aliases=aliases or {},
        compiler_params=pltpu.CompilerParams(vmem_limit_bytes=4 << 20),
        cost_estimate=pl.CostEstimate(flops=1, bytes_accessed=1, transcendentals=0),
        name=name,
    )(*[array for _, array in ins])


def chunks_of(columns):
    if columns % UNIT:
        return [(0, columns)]
    widths = [TARGET] * (columns // TARGET)
    if columns % TARGET:
        widths.append(columns % TARGET)
    return [(sum(widths[:index]), width) for index, width in enumerate(widths)]


class Work:
    def __init__(self, outer, high, matrix, row_factor, col_factor, col_mean, col_square, rows_total):
        self.outer, self.high, self.rows_total = outer, high, rows_total
        self.matrix, self.row = matrix, row_factor
        self.state = [col_factor, col_mean, col_square]
        self.rank = col_factor.shape[1]
        self.chunks = chunks_of(col_factor.shape[0])
        self.moved = {}
        self.new = {}
        self.grad = None

    def chunk(self, index):
        return (VMEM, (self.chunks[index][1], self.rank), F32)

    def first(self):
        rows, rank = self.row.shape
        width = self.chunks[0][1]
        wide = (VMEM, (rows, 2 * rank), BF16)
        self.twice, self.pair, self.turned, out = call(
            first_kernel, "first",
            [(SMEM, self.outer), (SMEM, self.high), (VMEM, self.row)]
            + [(VMEM, self.state[0][:width]), (VMEM, self.matrix[:, :width])],
            [wide, wide, (VMEM, (2 * rank, rows), BF16), self.chunk(0)],
        )
        return out

    def fresh(self, index, token):
        (out,) = call(
            functools.partial(fresh_kernel, self.chunks[index][0]), "fresh",
            [(ANY, token), (VMEM, self.twice), (VMEM, self.turned), (VMEM, self.state[0]), (VMEM, self.matrix)],
            [self.chunk(index)],
        )
        return out

    def middle(self, index, far, near, token):
        *self.moved[index], out = call(
            functools.partial(middle_kernel, self.chunks[index][0], self.rows_total), "middle",
            [(ANY, token), (SMEM, self.outer), (VMEM, far), (VMEM, near), (VMEM, self.twice), (VMEM, self.turned)]
            + [(VMEM, array) for array in (self.matrix, *self.state)],
            [self.chunk(index)] * 4,
        )
        return out

    def last(self, index, far, near, token):
        ins = [(ANY, token), (SMEM, self.outer), (VMEM, far), (VMEM, near), (VMEM, self.pair)]
        ins += [(VMEM, array) for array in (self.matrix, *self.moved[index])]
        begun = self.grad is not None
        if begun:
            ins += [(VMEM, self.grad)]
        self.new[index], self.grad = call(
            functools.partial(last_kernel, self.chunks[index][0], self.rows_total, begun), "last",
            ins,
            [self.chunk(index), (VMEM, self.row.shape, F32)],
            aliases={9: 1} if begun else None,
        )

    def new_cols(self, token):
        return call(
            store_kernel, "store",
            [(ANY, token)] + [(VMEM, self.new[index]) for index in range(len(self.chunks))],
            [(HBM, self.state[0].shape, F32), (VMEM, (8, self.rank), F32)],
            scratch=[pltpu.SemaphoreType.DMA((len(self.chunks),))],
        )


def plain_columns(work):
    every = range(len(work.chunks))
    sums = [lax.psum(work.first(), "row")]
    for index in every[1:]:
        sums.append(lax.psum(work.fresh(index, sums[0]), "row"))
    sums = [lax.psum(work.middle(index, sums[index], sums[index], sums[index]), "row") for index in every]
    for index in every:
        work.last(index, sums[index], sums[index], sums[index])


def join_sums_kernel(token_ref, own_ref, arrived_ref, out_ref):
    del token_ref
    out_ref[...] = own_ref[...] + arrived_ref[: out_ref.shape[0], :]


def merge_kernel(which, outer_ref, token_ref, *refs):
    del token_ref
    refs = dict(zip(which, refs, strict=True))
    outer = outer_ref[0] == 1
    if "whole" in refs:
        whole = refs["joined"][...] + refs["from_inner"][...]
        refs["whole"][...] = whole
        if "payload" in refs:
            own = refs["own"][...]
            low, high = sorted((own.shape[0], whole.shape[0]))
            refs["payload"][:low, :] = jnp.where(outer, own[:low], whole[:low])
            if high > low:
                refs["payload"][low:, :] = own[low:] if own.shape[0] == high else whole[low:]
    elif "payload" in refs:
        refs["payload"][...] = refs["own"][...]


def line_columns(work):
    n_col = lax.axis_size("col")
    outer_pairs = [(0, 1), (1, 0), (2, 3), (3, 2)]
    inner_pairs = []
    for col in range(n_col):
        inner_pairs += [(n_col + col, 2 * n_col + col), (2 * n_col + col, n_col + col)]
        inner_pairs += [(at * n_col + col, at * n_col + (col ^ 1)) for at in (0, 3)]
    chunks = len(work.chunks)
    slots = 2 * chunks
    own, joined, whole, from_outer, from_inner = {}, {}, {}, {}, {}
    own[0] = work.first()
    token = own[0]
    for k in range(slots + 3 * LAG):
        here, then, done = k - LAG, k - 2 * LAG, k - 3 * LAG
        if 0 <= here < slots:
            (joined[here],) = call(
                join_sums_kernel, "sum",
                [(ANY, token), (VMEM, own[here]), (VMEM, from_outer[here])],
                [work.chunk(here % chunks)],
            )
            token = joined[here]
            from_inner[k] = lax.ppermute(joined[here], ("row", "col"), inner_pairs)
        ins, outs = {}, {}
        if 0 <= then < slots:
            ins["joined"], ins["from_inner"] = joined[then], from_inner[here]
            outs["whole"] = work.chunk(then % chunks)
            if k < slots:
                ins["own"] = own[k]
                outs["payload"] = max(work.chunk(then % chunks), work.chunk(k % chunks), key=lambda o: o[1])
        if k < 2 * LAG:
            ins["own"], outs["payload"] = own[k], work.chunk(k)
        if outs:
            got = call(
                functools.partial(merge_kernel, [*ins, *outs]), "merge",
                [(SMEM, work.outer), (ANY, token)] + [(VMEM, array) for array in ins.values()],
                [*outs.values()],
            )
            got = dict(zip(outs, got, strict=True))
            token = got[[*outs][-1]]
            if "whole" in got:
                whole[then] = got["whole"]
        if k < slots + 2 * LAG:
            payload = got["payload"] if k < slots else whole[then]
            from_outer[k] = lax.ppermute(payload, "row", outer_pairs)
        nxt = k + 1
        if nxt < chunks:
            token = own[nxt] = work.fresh(nxt, token)
        elif nxt < slots:
            at = nxt - chunks
            token = own[nxt] = work.middle(at, from_outer[at + 2 * LAG], whole[at], token)
        if done >= chunks:
            work.last(done - chunks, from_outer[done + 2 * LAG], whole[done], token)
            token = work.grad


def row_step(work, row_mean, row_square, cols_total):
    high, grad = work.high, work.grad
    rows, rank = grad.shape
    half = (VMEM, (rows // 2, rank), F32)
    swap = [(0, 1), (1, 0), (2, 3), (3, 2)]
    across = [(0, 2), (2, 0), (1, 3), (3, 1)]
    keep, send = call(halves_kernel, "halves", [(SMEM, high), (VMEM, grad)], [half, half])
    part = keep + lax.ppermute(send, "col", swap)
    other = lax.ppermute(part, "col", across)
    new_cols, stored = work.new_cols(part)
    ins = [(VMEM, array) for array in (part, other, work.row, row_mean, row_square)]
    (new,) = call(
        functools.partial(row_kernel, cols_total), "row", [(ANY, stored), (SMEM, high), *ins], [half]
    )
    other = lax.ppermute(new, "col", swap)
    (out,) = call(
        join_kernel, "join",
        [(SMEM, high), (VMEM, new), (VMEM, other)],
        [(HBM, grad.shape, F32)],
        scratch=[pltpu.SemaphoreType.DMA((2,))],
    )
    return out, new_cols


def on_device(matrix, row_factor, col_factor, row_mean, row_square, col_mean, col_square):
    n_row = lax.axis_size("row")
    n_col = lax.axis_size("col")
    row, col = lax.axis_index("row"), lax.axis_index("col")
    outer = ((row == 0) | (row == n_row - 1)).astype(jnp.int32).reshape(1)
    high = (col & 1).astype(jnp.int32).reshape(1)
    work = Work(outer, high, matrix, row_factor, col_factor, col_mean, col_square, matrix.shape[0] * n_row)
    if n_row == 4 and n_col % 2 == 0:
        line_columns(work)
    else:
        plain_columns(work)
    cols_total = matrix.shape[1] * n_col
    if n_col == 4:
        new_rows, new_cols = row_step(work, row_mean, row_square, cols_total)
    else:
        new_cols, _ = work.new_cols(work.grad)
        summed = lax.psum(work.grad, "col")
        new_rows, _, _ = adam_move(row_factor, summed / cols_total, row_mean, row_square, START + 1)
    return new_rows, new_cols


def solution(mesh):
    return jax.shard_map(
        on_device,
        mesh=mesh,
        in_specs=(
            P(("grp", "row"), "col"),
            P(("grp", "row"), None),
            P(("grp", "col"), None),
            P(("grp", "row"), None),
            P(("grp", "row"), None),
            P(("grp", "col"), None),
            P(("grp", "col"), None),
        ),
        out_specs=(P(("grp", "row"), None), P(("grp", "col"), None)),
        check_vma=False,
    )
```

```python
import functools

import jax
import jax.numpy as jnp
from jax import lax
from jax.experimental import pallas as pl
from jax.experimental.pallas import tpu as pltpu
from jax.sharding import PartitionSpec as P

START = 100
DELTA = 1.0
LEARN_RATE = 0.05
BETA_ONE = 0.9
BETA_TWO = 0.999
EPSILON = 1e-08
F32, BF16 = jnp.float32, jnp.bfloat16
NT = (((1,), (1,)), ((), ()))
ROW_BLOCK = 256
UNIT = 128
TARGET = 256
OUTER_LAG = 3
INNER_LAG = 2
BATCH = 3


def adam_move(values, gradient, first_moment, square, counter):
    first_moment = BETA_ONE * first_moment + (1.0 - BETA_ONE) * gradient
    square = BETA_TWO * square + (1.0 - BETA_TWO) * gradient * gradient
    fixed_mean = first_moment / (1.0 - BETA_ONE**counter)
    fixed_square = square / (1.0 - BETA_TWO**counter)
    return (
        values - LEARN_RATE * fixed_mean / (jnp.sqrt(fixed_square) + EPSILON),
        first_moment,
        square,
    )


def split(values):
    high = values.astype(BF16)
    return high, (values - high.astype(F32)).astype(BF16)


def slopes_of(row_pair, col_pair, block):
    fitted = lax.dot_general(row_pair, col_pair, NT, preferred_element_type=F32)
    return jnp.clip(fitted - block.astype(F32), -DELTA, DELTA).astype(BF16)


def col_partial(twice_ref, turned_ref, col, mat_ref, first_col):
    col_pair = jnp.concatenate(split(col), axis=1)
    width, rank = col.shape
    total = None
    for at in range(0, mat_ref.shape[0], ROW_BLOCK):
        rows = pl.ds(at, ROW_BLOCK)
        slopes = slopes_of(twice_ref[rows, :], col_pair, mat_ref[rows, pl.ds(first_col, width)])
        term = jnp.dot(turned_ref[:, rows], slopes, preferred_element_type=F32)
        total = term if total is None else total + term
    return (total[:rank] + total[rank:]).T


def first_kernel(
    outer_ref, high_ref, row_hbm, col_hbm, mat_hbm, twice_ref, pair_ref, turned_ref, col_ref, mat_ref, out_ref,
    row_ref, sems,
):
    del outer_ref, high_ref
    width, columns = out_ref.shape[0], mat_ref.shape[1]
    loads = [
        pltpu.make_async_copy(row_hbm, row_ref, sems.at[0]),
        pltpu.make_async_copy(mat_hbm.at[:, pl.ds(0, width)], mat_ref.at[:, pl.ds(0, width)], sems.at[1]),
        pltpu.make_async_copy(col_hbm, col_ref, sems.at[2]),
    ]
    if width < columns:
        rest = pl.ds(width, columns - width)
        loads.append(pltpu.make_async_copy(mat_hbm.at[:, rest], mat_ref.at[:, rest], sems.at[3]))
    for load in loads:
        load.start()
    loads[0].wait()
    high, low = split(row_ref[...])
    twice_ref[...] = jnp.concatenate([high, high], axis=1)
    pair_ref[...] = jnp.concatenate([high, low], axis=1)
    turned_ref[...] = jnp.concatenate([high.T, low.T], axis=0)
    loads[1].wait()
    loads[2].wait()
    out_ref[...] = col_partial(twice_ref, turned_ref, col_ref[:width, :], mat_ref, 0)
    for load in loads[3:]:
        load.wait()


def pick(outer_ref, far_ref, near_ref):
    near = near_ref[...]
    return jnp.where(outer_ref[0] == 1, far_ref[: near.shape[0], :], near)


def fresh_kernel(at, token_ref, twice_ref, turned_ref, col_ref, mat_ref, out_ref):
    del token_ref
    width = out_ref.shape[0]
    col = col_ref[pl.ds(at, width), :]
    out_ref[...] = col_partial(twice_ref, turned_ref, col, mat_ref, at)


def middle_kernel(
    at, rows_total, token_ref, outer_ref, far_ref, near_ref, twice_ref, turned_ref, mat_ref, col_ref, mean_ref,
    square_ref, new_ref, new_mean_ref, new_square_ref, out_ref,
):
    del token_ref
    total = pick(outer_ref, far_ref, near_ref)
    own = pl.ds(at, out_ref.shape[0])
    new, new_mean_ref[...], new_square_ref[...] = adam_move(
        col_ref[own, :], total / rows_total, mean_ref[own, :], square_ref[own, :], START + 1
    )
    new_ref[...] = new
    out_ref[...] = col_partial(twice_ref, turned_ref, new, mat_ref, at)


def last_kernel(at, rows_total, count, token_ref, outer_ref, pair_ref, mat_ref, *refs):
    del token_ref
    out_ref, grad_ref, news = refs[-1], refs[5 * count : -1 - count], []
    for index in range(count):
        far_ref, near_ref, col_ref, mean_ref, square_ref = refs[5 * index : 5 * index + 5]
        gradient = pick(outer_ref, far_ref, near_ref) / rows_total
        new, _, _ = adam_move(col_ref[...], gradient, mean_ref[...], square_ref[...], START + 2)
        refs[index - 1 - count][...] = new
        news.append(new)
    high, low = split(jnp.concatenate(news, axis=0))
    twice = jnp.concatenate([high, high], axis=1)
    pair = jnp.concatenate([high, low], axis=1)
    width, rank = high.shape
    for at_row in range(0, mat_ref.shape[0], ROW_BLOCK):
        rows = pl.ds(at_row, ROW_BLOCK)
        slopes = slopes_of(pair_ref[rows, :], twice, mat_ref[rows, pl.ds(at, width)])
        term = jnp.dot(slopes, pair, preferred_element_type=F32)
        term = term[:, :rank] + term[:, rank:]
        out_ref[rows, :] = grad_ref[0][rows, :] + term if grad_ref else term


def store_kernel(token_ref, *refs):
    del token_ref
    *chunk_refs, out_hbm, done_ref, sems = refs
    done_ref[...] = jnp.zeros_like(done_ref)
    stores, at = [], 0
    for index, chunk_ref in enumerate(chunk_refs):
        target = out_hbm.at[pl.ds(at, chunk_ref.shape[0]), :]
        stores.append(pltpu.make_async_copy(chunk_ref, target, sems.at[index]))
        at += chunk_ref.shape[0]
    for store in stores:
        store.start()
    for store in stores:
        store.wait()


def halves_kernel(high_ref, grad_ref, keep_ref, send_ref):
    half = keep_ref.shape[0]
    keep_ref[...] = grad_ref[pl.ds(pl.multiple_of(high_ref[0] * half, half), half), :]
    send_ref[...] = grad_ref[pl.ds(pl.multiple_of((1 - high_ref[0]) * half, half), half), :]


def row_kernel(cols_total, token_ref, high_ref, part_ref, other_ref, row_ref, mean_ref, square_ref, new_ref):
    del token_ref
    half = part_ref.shape[0]
    own = pl.ds(pl.multiple_of(high_ref[0] * half, half), half)
    gradient = (part_ref[...] + other_ref[...]) / cols_total
    new_ref[...], _, _ = adam_move(row_ref[own, :], gradient, mean_ref[own, :], square_ref[own, :], START + 1)


def join_kernel(high_ref, new_ref, other_ref, out_hbm, sems):
    half = new_ref.shape[0]
    own = pl.multiple_of(high_ref[0] * half, half)
    far = pl.multiple_of((1 - high_ref[0]) * half, half)
    stores = [
        pltpu.make_async_copy(new_ref, out_hbm.at[pl.ds(own, half), :], sems.at[0]),
        pltpu.make_async_copy(other_ref, out_hbm.at[pl.ds(far, half), :], sems.at[1]),
    ]
    for store in stores:
        store.start()
    for store in stores:
        store.wait()


VMEM = pl.BlockSpec(memory_space=pltpu.VMEM)
SMEM = pl.BlockSpec(memory_space=pltpu.SMEM)
ANY = pl.BlockSpec(memory_space=pl.ANY)
HBM = pl.BlockSpec(memory_space=pltpu.HBM)


def call(kernel, name, ins, outs, scratch=(), aliases=None, room=4):
    return pl.pallas_call(
        kernel,
        out_shape=[jax.ShapeDtypeStruct(shape, kind) for _, shape, kind in outs],
        in_specs=[spec for spec, _ in ins],
        out_specs=[spec for spec, _, _ in outs],
        scratch_shapes=scratch,
        input_output_aliases=aliases or {},
        compiler_params=pltpu.CompilerParams(vmem_limit_bytes=room << 20),
        cost_estimate=pl.CostEstimate(flops=1, bytes_accessed=1, transcendentals=0),
        name=name,
    )(*[pltpu.with_memory_space_constraint(array, pltpu.HBM) if spec is HBM else array for spec, array in ins])


def chunks_of(columns):
    if columns % UNIT:
        return [(0, columns)]
    widths = [TARGET] * (columns // TARGET)
    if columns % TARGET:
        widths.append(columns % TARGET)
    return [(sum(widths[:index]), width) for index, width in enumerate(widths)]


class Work:
    def __init__(self, outer, high, matrix, row_factor, col_factor, col_mean, col_square, rows_total):
        self.outer, self.high, self.rows_total = outer, high, rows_total
        self.matrix, self.row = matrix, row_factor
        self.state = [col_factor, col_mean, col_square]
        self.rank = col_factor.shape[1]
        self.chunks = chunks_of(col_factor.shape[0])
        self.moved = {}
        self.new = {}
        self.grad = None

    def chunk(self, index):
        return (VMEM, (self.chunks[index][1], self.rank), F32)

    def first(self):
        rows, rank = self.row.shape
        wide = (VMEM, (rows, 2 * rank), BF16)
        col = self.state[0]
        self.twice, self.pair, self.turned, self.state[0], self.matrix, out = call(
            first_kernel, "first",
            [(SMEM, self.outer), (SMEM, self.high), (HBM, self.row), (HBM, col), (HBM, self.matrix)],
            [wide, wide, (VMEM, (2 * rank, rows), BF16)]
            + [(VMEM, col.shape, F32), (VMEM, self.matrix.shape, BF16), self.chunk(0)],
            scratch=[pltpu.VMEM(self.row.shape, F32), pltpu.SemaphoreType.DMA((4,))],
            room=4,
        )
        return out

    def fresh(self, index, token):
        (out,) = call(
            functools.partial(fresh_kernel, self.chunks[index][0]), "fresh",
            [(ANY, token), (VMEM, self.twice), (VMEM, self.turned), (VMEM, self.state[0]), (VMEM, self.matrix)],
            [self.chunk(index)],
        )
        return out

    def middle(self, index, far, near, token):
        *self.moved[index], out = call(
            functools.partial(middle_kernel, self.chunks[index][0], self.rows_total), "middle",
            [(ANY, token), (SMEM, self.outer), (VMEM, far), (VMEM, near), (VMEM, self.twice), (VMEM, self.turned)]
            + [(VMEM, array) for array in (self.matrix, *self.state)],
            [self.chunk(index)] * 4,
        )
        return out

    def last(self, indices, far, near, token):
        ins = [(ANY, token), (SMEM, self.outer), (VMEM, self.pair), (VMEM, self.matrix)]
        for index in indices:
            ins += [(VMEM, array) for array in (far[index], near[index], *self.moved[index])]
        aliases = None
        if self.grad is not None:
            aliases = {len(ins): len(indices)}
            ins.append((VMEM, self.grad))
        *new, self.grad = call(
            functools.partial(last_kernel, self.chunks[indices[0]][0], self.rows_total, len(indices)), "last",
            ins,
            [*map(self.chunk, indices), (VMEM, self.row.shape, F32)],
            aliases=aliases,
        )
        self.new.update(zip(indices, new, strict=True))

    def new_cols(self, token):
        return call(
            store_kernel, "store",
            [(ANY, token)] + [(VMEM, self.new[index]) for index in range(len(self.chunks))],
            [(HBM, self.state[0].shape, F32), (VMEM, (8, self.rank), F32)],
            scratch=[pltpu.SemaphoreType.DMA((len(self.chunks),))],
        )


def plain_columns(work):
    every = range(len(work.chunks))
    sums = [lax.psum(work.first(), "row")]
    for index in every[1:]:
        sums.append(lax.psum(work.fresh(index, sums[0]), "row"))
    sums = [lax.psum(work.middle(index, sums[index], sums[index], sums[index]), "row") for index in every]
    for index in every:
        work.last([index], sums, sums, sums[index])


def join_sums_kernel(token_ref, own_ref, arrived_ref, out_ref):
    del token_ref
    out_ref[...] = own_ref[...] + arrived_ref[: out_ref.shape[0], :]


def merge_kernel(which, outer_ref, token_ref, *refs):
    del token_ref
    refs = dict(zip(which, refs, strict=True))
    outer = outer_ref[0] == 1
    if "whole" in refs:
        whole = refs["joined"][...] + refs["from_inner"][...]
        refs["whole"][...] = whole
        if "payload" in refs:
            own = refs["own"][...]
            low, high = sorted((own.shape[0], whole.shape[0]))
            refs["payload"][:low, :] = jnp.where(outer, own[:low], whole[:low])
            if high > low:
                refs["payload"][low:, :] = own[low:] if own.shape[0] == high else whole[low:]
    elif "payload" in refs:
        refs["payload"][...] = refs["own"][...]


def line_columns(work):
    n_col = lax.axis_size("col")
    outer_pairs = [(0, 1), (1, 0), (2, 3), (3, 2)]
    inner_pairs = []
    for col in range(n_col):
        inner_pairs += [(n_col + col, 2 * n_col + col), (2 * n_col + col, n_col + col)]
        inner_pairs += [(at * n_col + col, at * n_col + (col ^ 1)) for at in (0, 3)]
    chunks = len(work.chunks)
    slots = 2 * chunks
    own, joined, whole, from_outer, from_inner = {}, {}, {}, {}, {}
    far, near, pending = {}, {}, []
    own[0] = work.first()
    token = own[0]
    for k in range(slots + 2 * OUTER_LAG + INNER_LAG):
        here = k - OUTER_LAG
        then = here - INNER_LAG
        done = then - OUTER_LAG
        if 0 <= here < slots:
            (joined[here],) = call(
                join_sums_kernel, "sum",
                [(ANY, token), (VMEM, own[here]), (VMEM, from_outer[here])],
                [work.chunk(here % chunks)],
            )
            token = joined[here]
            from_inner[k] = lax.ppermute(joined[here], ("row", "col"), inner_pairs)
        ins, outs = {}, {}
        if 0 <= then < slots:
            ins["joined"], ins["from_inner"] = joined[then], from_inner[k - INNER_LAG]
            outs["whole"] = work.chunk(then % chunks)
            if k < slots:
                ins["own"] = own[k]
                outs["payload"] = max(work.chunk(then % chunks), work.chunk(k % chunks), key=lambda o: o[1])
        if k < OUTER_LAG + INNER_LAG:
            ins["own"], outs["payload"] = own[k], work.chunk(k)
        if outs:
            got = call(
                functools.partial(merge_kernel, [*ins, *outs]), "merge",
                [(SMEM, work.outer), (ANY, token)] + [(VMEM, array) for array in ins.values()],
                [*outs.values()],
            )
            got = dict(zip(outs, got, strict=True))
            token = got[[*outs][-1]]
            if "whole" in got:
                whole[then] = got["whole"]
        if k < slots + OUTER_LAG + INNER_LAG:
            payload = got["payload"] if k < slots else whole[then]
            from_outer[k] = lax.ppermute(payload, "row", outer_pairs)
        nxt = k + 1
        if nxt < chunks:
            token = own[nxt] = work.fresh(nxt, token)
        elif nxt < slots:
            at = nxt - chunks
            token = own[nxt] = work.middle(at, from_outer[at + OUTER_LAG + INNER_LAG], whole[at], token)
        if done >= chunks:
            at = done - chunks
            far[at], near[at] = from_outer[done + OUTER_LAG + INNER_LAG], whole[done]
            pending.append(at)
        if pending and nxt >= slots:
            batch, pending = pending[:BATCH], pending[BATCH:]
            work.last(batch, far, near, token)
            token = work.grad


def row_step(work, row_mean, row_square, cols_total):
    high, grad = work.high, work.grad
    rows, rank = grad.shape
    half = (VMEM, (rows // 2, rank), F32)
    swap = [(0, 1), (1, 0), (2, 3), (3, 2)]
    across = [(0, 2), (2, 0), (1, 3), (3, 1)]
    keep, send = call(halves_kernel, "halves", [(SMEM, high), (VMEM, grad)], [half, half])
    part = keep + lax.ppermute(send, "col", swap)
    other = lax.ppermute(part, "col", across)
    new_cols, stored = work.new_cols(part)
    ins = [(VMEM, array) for array in (part, other, work.row, row_mean, row_square)]
    (new,) = call(
        functools.partial(row_kernel, cols_total), "row", [(ANY, stored), (SMEM, high), *ins], [half]
    )
    other = lax.ppermute(new, "col", swap)
    (out,) = call(
        join_kernel, "join",
        [(SMEM, high), (VMEM, new), (VMEM, other)],
        [(HBM, grad.shape, F32)],
        scratch=[pltpu.SemaphoreType.DMA((2,))],
    )
    return out, new_cols


def on_device(matrix, row_factor, col_factor, row_mean, row_square, col_mean, col_square):
    n_row = lax.axis_size("row")
    n_col = lax.axis_size("col")
    row, col = lax.axis_index("row"), lax.axis_index("col")
    outer = ((row == 0) | (row == n_row - 1)).astype(jnp.int32).reshape(1)
    high = (col & 1).astype(jnp.int32).reshape(1)
    work = Work(outer, high, matrix, row_factor, col_factor, col_mean, col_square, matrix.shape[0] * n_row)
    if n_row == 4 and n_col % 2 == 0:
        line_columns(work)
    else:
        plain_columns(work)
    cols_total = matrix.shape[1] * n_col
    if n_col == 4:
        new_rows, new_cols = row_step(work, row_mean, row_square, cols_total)
    else:
        new_cols, _ = work.new_cols(work.grad)
        summed = lax.psum(work.grad, "col")
        new_rows, _, _ = adam_move(row_factor, summed / cols_total, row_mean, row_square, START + 1)
    return new_rows, new_cols


def solution(mesh):
    return jax.shard_map(
        on_device,
        mesh=mesh,
        in_specs=(
            P(("grp", "row"), "col"),
            P(("grp", "row"), None),
            P(("grp", "col"), None),
            P(("grp", "row"), None),
            P(("grp", "row"), None),
            P(("grp", "col"), None),
            P(("grp", "col"), None),
        ),
        out_specs=(P(("grp", "row"), None), P(("grp", "col"), None)),
        check_vma=False,
    )
```

```python
import functools

import jax
import jax.numpy as jnp
from jax import lax
from jax.experimental import pallas as pl
from jax.experimental.pallas import tpu as pltpu
from jax.sharding import PartitionSpec as P

START = 100
DELTA = 1.0
LEARN_RATE = 0.05
BETA_ONE = 0.9
BETA_TWO = 0.999
EPSILON = 1e-08
F32, BF16 = jnp.float32, jnp.bfloat16
NT = (((1,), (1,)), ((), ()))
ROW_BLOCK = 1024
UNIT = 128
TARGET = 256
OUTER_LAG = 3
INNER_LAG = 2
BATCH = 3


def adam_move(values, gradient, first_moment, square, counter):
    first_moment = BETA_ONE * first_moment + (1.0 - BETA_ONE) * gradient
    square = BETA_TWO * square + (1.0 - BETA_TWO) * gradient * gradient
    fixed_mean = first_moment / (1.0 - BETA_ONE**counter)
    fixed_square = square / (1.0 - BETA_TWO**counter)
    return (
        values - LEARN_RATE * fixed_mean / (jnp.sqrt(fixed_square) + EPSILON),
        first_moment,
        square,
    )


def split(values):
    high = values.astype(BF16)
    return high, (values - high.astype(F32)).astype(BF16)


def slopes_of(row_pair, col_pair, block):
    fitted = lax.dot_general(row_pair, col_pair, NT, preferred_element_type=F32)
    return jnp.clip(fitted - block.astype(F32), -DELTA, DELTA).astype(BF16)


def col_partial(twice_ref, turned_ref, col, mat_ref, first_col):
    col_pair = jnp.concatenate(split(col), axis=1)
    width, rank = col.shape
    total = None
    for at in range(0, mat_ref.shape[0], ROW_BLOCK):
        rows = pl.ds(at, ROW_BLOCK)
        slopes = slopes_of(twice_ref[rows, :], col_pair, mat_ref[rows, pl.ds(first_col, width)])
        term = jnp.dot(turned_ref[:, rows], slopes, preferred_element_type=F32)
        total = term if total is None else total + term
    return (total[:rank] + total[rank:]).T


def first_kernel(
    outer_ref, high_ref, row_hbm, col_hbm, mat_hbm, twice_ref, pair_ref, turned_ref, one_ref, two_ref,
    row_ref, col_ref, mat_ref, sems,
):
    del outer_ref, high_ref
    width = col_ref.shape[0]
    loads = [
        pltpu.make_async_copy(row_hbm, row_ref, sems.at[0]),
        pltpu.make_async_copy(mat_hbm.at[:, pl.ds(0, width)], mat_ref, sems.at[1]),
        pltpu.make_async_copy(col_hbm.at[pl.ds(0, width), :], col_ref, sems.at[2]),
    ]
    for load in loads:
        load.start()
    loads[0].wait()
    high, low = split(row_ref[...])
    twice_ref[...] = jnp.concatenate([high, high], axis=1)
    pair_ref[...] = jnp.concatenate([high, low], axis=1)
    turned_ref[...] = jnp.concatenate([high.T, low.T], axis=0)
    loads[1].wait()
    loads[2].wait()
    out = col_partial(twice_ref, turned_ref, col_ref[...], mat_ref, 0)
    one_ref[...] = out[: one_ref.shape[0]]
    two_ref[...] = out[one_ref.shape[0] :]


def third_kernel(
    at, token_ref, col_hbm, mat_hbm, twice_ref, turned_ref, col_ref, mat_ref, out_ref, sems
):
    del token_ref
    width, columns = out_ref.shape[0], mat_ref.shape[1]
    soon = at + width
    loads = [
        pltpu.make_async_copy(mat_hbm.at[:, pl.ds(0, soon)], mat_ref.at[:, pl.ds(0, soon)], sems.at[0]),
        pltpu.make_async_copy(col_hbm, col_ref, sems.at[1]),
    ]
    if soon < columns:
        rest = pl.ds(soon, columns - soon)
        loads.append(pltpu.make_async_copy(mat_hbm.at[:, rest], mat_ref.at[:, rest], sems.at[2]))
    for load in loads:
        load.start()
    loads[0].wait()
    loads[1].wait()
    col = col_ref[pl.ds(at, width), :]
    out_ref[...] = col_partial(twice_ref, turned_ref, col, mat_ref, at)
    for load in loads[2:]:
        load.wait()


def pick(outer_ref, far_ref, near_ref):
    near = near_ref[...]
    return jnp.where(outer_ref[0] == 1, far_ref[: near.shape[0], :], near)


def pick_kernel(outer_ref, token_ref, far_ref, near_ref, out_ref):
    del token_ref
    out_ref[...] = pick(outer_ref, far_ref, near_ref)


def fresh_kernel(at, token_ref, twice_ref, turned_ref, col_ref, mat_ref, out_ref):
    del token_ref
    width = out_ref.shape[0]
    col = col_ref[pl.ds(at, width), :]
    out_ref[...] = col_partial(twice_ref, turned_ref, col, mat_ref, at)


def middle_kernel(
    at, rows_total, token_ref, outer_ref, far_ref, near_ref, twice_ref, turned_ref, mat_ref, col_ref, mean_ref,
    square_ref, new_ref, new_mean_ref, new_square_ref, out_ref,
):
    del token_ref
    total = pick(outer_ref, far_ref, near_ref)
    own = pl.ds(at, out_ref.shape[0])
    new, new_mean_ref[...], new_square_ref[...] = adam_move(
        col_ref[own, :], total / rows_total, mean_ref[own, :], square_ref[own, :], START + 1
    )
    new_ref[...] = new
    out_ref[...] = col_partial(twice_ref, turned_ref, new, mat_ref, at)


def last_kernel(at, rows_total, count, token_ref, outer_ref, pair_ref, mat_ref, *refs):
    del token_ref
    out_ref, grad_ref, news = refs[-1], refs[5 * count : -1 - count], []
    for index in range(count):
        far_ref, near_ref, col_ref, mean_ref, square_ref = refs[5 * index : 5 * index + 5]
        gradient = pick(outer_ref, far_ref, near_ref) / rows_total
        new, _, _ = adam_move(col_ref[...], gradient, mean_ref[...], square_ref[...], START + 2)
        refs[index - 1 - count][...] = new
        news.append(new)
    high, low = split(jnp.concatenate(news, axis=0))
    twice = jnp.concatenate([high, high], axis=1)
    pair = jnp.concatenate([high, low], axis=1)
    width, rank = high.shape
    for at_row in range(0, mat_ref.shape[0], ROW_BLOCK):
        rows = pl.ds(at_row, ROW_BLOCK)
        slopes = slopes_of(pair_ref[rows, :], twice, mat_ref[rows, pl.ds(at, width)])
        term = jnp.dot(slopes, pair, preferred_element_type=F32)
        term = term[:, :rank] + term[:, rank:]
        out_ref[rows, :] = grad_ref[0][rows, :] + term if grad_ref else term


def store_kernel(token_ref, *refs):
    del token_ref
    *chunk_refs, out_hbm, done_ref, sems = refs
    done_ref[...] = jnp.zeros_like(done_ref)
    stores, at = [], 0
    for index, chunk_ref in enumerate(chunk_refs):
        target = out_hbm.at[pl.ds(at, chunk_ref.shape[0]), :]
        stores.append(pltpu.make_async_copy(chunk_ref, target, sems.at[index]))
        at += chunk_ref.shape[0]
    for store in stores:
        store.start()
    for store in stores:
        store.wait()


def halves_kernel(high_ref, grad_ref, keep_ref, send_ref):
    half = keep_ref.shape[0]
    keep_ref[...] = grad_ref[pl.ds(pl.multiple_of(high_ref[0] * half, half), half), :]
    send_ref[...] = grad_ref[pl.ds(pl.multiple_of((1 - high_ref[0]) * half, half), half), :]


def row_kernel(cols_total, token_ref, high_ref, part_ref, other_ref, row_ref, mean_ref, square_ref, new_ref):
    del token_ref
    half = part_ref.shape[0]
    own = pl.ds(pl.multiple_of(high_ref[0] * half, half), half)
    gradient = (part_ref[...] + other_ref[...]) / cols_total
    new_ref[...], _, _ = adam_move(row_ref[own, :], gradient, mean_ref[own, :], square_ref[own, :], START + 1)


def join_kernel(high_ref, new_ref, other_ref, out_hbm, sems):
    half = new_ref.shape[0]
    own = pl.multiple_of(high_ref[0] * half, half)
    far = pl.multiple_of((1 - high_ref[0]) * half, half)
    stores = [
        pltpu.make_async_copy(new_ref, out_hbm.at[pl.ds(own, half), :], sems.at[0]),
        pltpu.make_async_copy(other_ref, out_hbm.at[pl.ds(far, half), :], sems.at[1]),
    ]
    for store in stores:
        store.start()
    for store in stores:
        store.wait()


VMEM = pl.BlockSpec(memory_space=pltpu.VMEM)
SMEM = pl.BlockSpec(memory_space=pltpu.SMEM)
ANY = pl.BlockSpec(memory_space=pl.ANY)
HBM = pl.BlockSpec(memory_space=pltpu.HBM)


def call(kernel, name, ins, outs, scratch=(), aliases=None):
    return pl.pallas_call(
        kernel,
        out_shape=[jax.ShapeDtypeStruct(shape, kind) for _, shape, kind in outs],
        in_specs=[spec for spec, _ in ins],
        out_specs=[spec for spec, _, _ in outs],
        scratch_shapes=scratch,
        input_output_aliases=aliases or {},
        compiler_params=pltpu.CompilerParams(vmem_limit_bytes=6 << 20),
        cost_estimate=pl.CostEstimate(flops=1, bytes_accessed=1, transcendentals=0),
        name=name,
    )(*[pltpu.with_memory_space_constraint(array, pltpu.HBM) if spec is HBM else array for spec, array in ins])


def chunks_of(columns):
    widths = [TARGET] * (columns // TARGET)
    if columns % TARGET:
        widths.append(columns % TARGET)
    return [(sum(widths[:index]), width) for index, width in enumerate(widths)]


class Work:
    def __init__(self, outer, high, matrix, row_factor, col_factor, col_mean, col_square, rows_total):
        self.outer, self.high, self.rows_total = outer, high, rows_total
        self.matrix, self.row = matrix, row_factor
        self.state = [col_factor, col_mean, col_square]
        self.rank = col_factor.shape[1]
        self.chunks = chunks_of(col_factor.shape[0])
        self.moved = {}
        self.new = {}
        self.grad = None

    def chunk(self, index):
        return (VMEM, (self.chunks[index][1], self.rank), F32)

    def first(self):
        rows, rank = self.row.shape
        width = sum(self.chunks[1])
        wide = (VMEM, (rows, 2 * rank), BF16)
        self.twice, self.pair, self.turned, out, self.early = call(
            first_kernel, "first",
            [(SMEM, self.outer), (SMEM, self.high), (HBM, self.row), (HBM, self.state[0]), (HBM, self.matrix)],
            [wide, wide, (VMEM, (2 * rank, rows), BF16), self.chunk(0), self.chunk(1)],
            scratch=[
                pltpu.VMEM(self.row.shape, F32),
                pltpu.VMEM((width, rank), F32),
                pltpu.VMEM((rows, width), BF16),
                pltpu.SemaphoreType.DMA((3,)),
            ],
        )
        return out

    def third(self, token):
        col = self.state[0]
        self.state[0], self.matrix, out = call(
            functools.partial(third_kernel, self.chunks[2][0]), "third",
            [(ANY, token), (HBM, col), (HBM, self.matrix), (VMEM, self.twice), (VMEM, self.turned)],
            [(VMEM, col.shape, F32), (VMEM, self.matrix.shape, BF16), self.chunk(2)],
            scratch=[pltpu.SemaphoreType.DMA((3,))],
        )
        return out

    def fresh(self, index, token):
        if index == 1:
            return self.early
        if index == 2:
            return self.third(token)
        (out,) = call(
            functools.partial(fresh_kernel, self.chunks[index][0]), "fresh",
            [(ANY, token), (VMEM, self.twice), (VMEM, self.turned), (VMEM, self.state[0]), (VMEM, self.matrix)],
            [self.chunk(index)],
        )
        return out

    def middle(self, index, far, near, token):
        *self.moved[index], out = call(
            functools.partial(middle_kernel, self.chunks[index][0], self.rows_total), "middle",
            [(ANY, token), (SMEM, self.outer), (VMEM, far), (VMEM, near), (VMEM, self.twice), (VMEM, self.turned)]
            + [(VMEM, array) for array in (self.matrix, *self.state)],
            [self.chunk(index)] * 4,
        )
        return out

    def last(self, indices, far, near, token):
        ins = [(ANY, token), (SMEM, self.outer), (VMEM, self.pair), (VMEM, self.matrix)]
        for index in indices:
            ins += [(VMEM, array) for array in (far[index], near[index], *self.moved[index])]
        aliases = None
        if self.grad is not None:
            aliases = {len(ins): len(indices)}
            ins.append((VMEM, self.grad))
        *new, self.grad = call(
            functools.partial(last_kernel, self.chunks[indices[0]][0], self.rows_total, len(indices)), "last",
            ins,
            [*map(self.chunk, indices), (VMEM, self.row.shape, F32)],
            aliases=aliases,
        )
        self.new.update(zip(indices, new, strict=True))

    def new_cols(self, token):
        return call(
            store_kernel, "store",
            [(ANY, token)] + [(VMEM, self.new[index]) for index in range(len(self.chunks))],
            [(HBM, self.state[0].shape, F32), (VMEM, (8, self.rank), F32)],
            scratch=[pltpu.SemaphoreType.DMA((len(self.chunks),))],
        )


def plain_columns(work):
    every = range(len(work.chunks))
    sums = [lax.psum(work.first(), "row")]
    for index in every[1:]:
        sums.append(lax.psum(work.fresh(index, sums[0]), "row"))
    sums = [lax.psum(work.middle(index, sums[index], sums[index], sums[index]), "row") for index in every]
    for index in every:
        work.last([index], sums, sums, sums[index])


def join_sums_kernel(token_ref, own_ref, arrived_ref, out_ref):
    del token_ref
    out_ref[...] = own_ref[...] + arrived_ref[: out_ref.shape[0], :]


def merge_kernel(which, outer_ref, token_ref, *refs):
    del token_ref
    refs = dict(zip(which, refs, strict=True))
    outer = outer_ref[0] == 1
    if "whole" in refs:
        whole = refs["joined"][...] + refs["from_inner"][...]
        refs["whole"][...] = whole
        if "payload" in refs:
            own = refs["own"][...]
            low, high = sorted((own.shape[0], whole.shape[0]))
            refs["payload"][:low, :] = jnp.where(outer, own[:low], whole[:low])
            if high > low:
                refs["payload"][low:, :] = own[low:] if own.shape[0] == high else whole[low:]
    elif "payload" in refs:
        refs["payload"][...] = refs["own"][...]


def line_columns(work):
    n_col = lax.axis_size("col")
    outer_pairs = [(0, 1), (1, 0), (2, 3), (3, 2)]
    inner_pairs = []
    for col in range(n_col):
        inner_pairs += [(n_col + col, 2 * n_col + col), (2 * n_col + col, n_col + col)]
        inner_pairs += [(at * n_col + col, at * n_col + (col ^ 1)) for at in (0, 3)]
    chunks = len(work.chunks)
    slots = 2 * chunks
    own, joined, whole, from_outer, from_inner = {}, {}, {}, {}, {}
    far, near, pending = {}, {}, []
    own[0] = work.first()
    token = own[0]
    for k in range(slots + 2 * OUTER_LAG + INNER_LAG):
        here = k - OUTER_LAG
        then = here - INNER_LAG
        done = then - OUTER_LAG
        if 0 <= here < slots:
            (joined[here],) = call(
                join_sums_kernel, "sum",
                [(ANY, token), (VMEM, own[here]), (VMEM, from_outer[here])],
                [work.chunk(here % chunks)],
            )
            token = joined[here]
            from_inner[k] = lax.ppermute(joined[here], ("row", "col"), inner_pairs)
        ins, outs = {}, {}
        if 0 <= then < slots:
            ins["joined"], ins["from_inner"] = joined[then], from_inner[k - INNER_LAG]
            outs["whole"] = work.chunk(then % chunks)
            if k < slots:
                ins["own"] = own[k]
                outs["payload"] = max(work.chunk(then % chunks), work.chunk(k % chunks), key=lambda o: o[1])
        if k < OUTER_LAG + INNER_LAG:
            ins["own"], outs["payload"] = own[k], work.chunk(k)
        if outs:
            got = call(
                functools.partial(merge_kernel, [*ins, *outs]), "merge",
                [(SMEM, work.outer), (ANY, token)] + [(VMEM, array) for array in ins.values()],
                [*outs.values()],
            )
            got = dict(zip(outs, got, strict=True))
            token = got[[*outs][-1]]
            if "whole" in got:
                whole[then] = got["whole"]
        if k < slots + OUTER_LAG + INNER_LAG:
            payload = got["payload"] if k < slots else whole[then]
            from_outer[k] = lax.ppermute(payload, "row", outer_pairs)
        early = k - 2 * OUTER_LAG - INNER_LAG + 1
        if 11 <= early - chunks < chunks:
            at = early - chunks
            (token,) = call(
                pick_kernel, "pick",
                [(SMEM, work.outer), (ANY, token), (VMEM, from_outer[k - OUTER_LAG + 1]), (VMEM, whole[early])],
                [work.chunk(at)],
            )
            far[at] = near[at] = token
        nxt = k + 1
        if nxt < chunks:
            token = own[nxt] = work.fresh(nxt, token)
        elif nxt < slots:
            at = nxt - chunks
            token = own[nxt] = work.middle(at, from_outer[at + OUTER_LAG + INNER_LAG], whole[at], token)
        if done >= chunks:
            at = done - chunks
            if at not in far:
                far[at], near[at] = from_outer[done + OUTER_LAG + INNER_LAG], whole[done]
            pending.append(at)
        if pending and nxt >= slots:
            count = BATCH if done + 1 < slots else len(pending)
            batch, pending = pending[:count], pending[count:]
            work.last(batch, far, near, token)
            token = work.grad


def row_step(work, row_mean, row_square, cols_total):
    high, grad = work.high, work.grad
    rows, rank = grad.shape
    half = (VMEM, (rows // 2, rank), F32)
    swap = [(0, 1), (1, 0), (2, 3), (3, 2)]
    across = [(0, 2), (2, 0), (1, 3), (3, 1)]
    keep, send = call(halves_kernel, "halves", [(SMEM, high), (VMEM, grad)], [half, half])
    part = keep + lax.ppermute(send, "col", swap)
    other = lax.ppermute(part, "col", across)
    new_cols, stored = work.new_cols(part)
    ins = [(VMEM, array) for array in (part, other, work.row, row_mean, row_square)]
    (new,) = call(
        functools.partial(row_kernel, cols_total), "row", [(ANY, stored), (SMEM, high), *ins], [half]
    )
    other = lax.ppermute(new, "col", swap)
    (out,) = call(
        join_kernel, "join",
        [(SMEM, high), (VMEM, new), (VMEM, other)],
        [(HBM, grad.shape, F32)],
        scratch=[pltpu.SemaphoreType.DMA((2,))],
    )
    return out, new_cols


def on_device(matrix, row_factor, col_factor, row_mean, row_square, col_mean, col_square):
    n_row = lax.axis_size("row")
    n_col = lax.axis_size("col")
    row, col = lax.axis_index("row"), lax.axis_index("col")
    outer = ((row == 0) | (row == n_row - 1)).astype(jnp.int32).reshape(1)
    high = (col & 1).astype(jnp.int32).reshape(1)
    work = Work(outer, high, matrix, row_factor, col_factor, col_mean, col_square, matrix.shape[0] * n_row)
    if n_row == 4 and n_col % 2 == 0:
        line_columns(work)
    else:
        plain_columns(work)
    cols_total = matrix.shape[1] * n_col
    if n_col == 4:
        new_rows, new_cols = row_step(work, row_mean, row_square, cols_total)
    else:
        new_cols, _ = work.new_cols(work.grad)
        summed = lax.psum(work.grad, "col")
        new_rows, _, _ = adam_move(row_factor, summed / cols_total, row_mean, row_square, START + 1)
    return new_rows, new_cols


def solution(mesh):
    return jax.shard_map(
        on_device,
        mesh=mesh,
        in_specs=(
            P(("grp", "row"), "col"),
            P(("grp", "row"), None),
            P(("grp", "col"), None),
            P(("grp", "row"), None),
            P(("grp", "row"), None),
            P(("grp", "col"), None),
            P(("grp", "col"), None),
        ),
        out_specs=(P(("grp", "row"), None), P(("grp", "col"), None)),
        check_vma=False,
    )
```

```python
import functools

import jax
import jax.numpy as jnp
from jax import lax
from jax.experimental import pallas as pl
from jax.experimental.pallas import tpu as pltpu
from jax.sharding import PartitionSpec as P

START = 100
DELTA = 1.0
LEARN_RATE = 0.05
BETA_ONE = 0.9
BETA_TWO = 0.999
EPSILON = 1e-08
F32, BF16 = jnp.float32, jnp.bfloat16
NT = (((1,), (1,)), ((), ()))
ROW_BLOCK = 1024
UNIT = 128
TARGET = 256
OUTER_LAG = 3
INNER_LAG = 2
BATCH = 3


def adam_move(values, gradient, first_moment, square, counter):
    first_moment = BETA_ONE * first_moment + (1.0 - BETA_ONE) * gradient
    square = BETA_TWO * square + (1.0 - BETA_TWO) * gradient * gradient
    fixed_mean = first_moment / (1.0 - BETA_ONE**counter)
    fixed_square = square / (1.0 - BETA_TWO**counter)
    return (
        values - LEARN_RATE * fixed_mean / (jnp.sqrt(fixed_square) + EPSILON),
        first_moment,
        square,
    )


def split(values):
    high = values.astype(BF16)
    return high, (values - high.astype(F32)).astype(BF16)


def slopes_of(row_pair, col_pair, block):
    fitted = lax.dot_general(row_pair, col_pair, NT, preferred_element_type=F32)
    return jnp.clip(fitted - block.astype(F32), -DELTA, DELTA).astype(BF16)


def col_partial(twice_ref, turned_ref, col, mat_ref, first_col):
    col_pair = jnp.concatenate(split(col), axis=1)
    width, rank = col.shape
    total = None
    for at in range(0, mat_ref.shape[0], ROW_BLOCK):
        rows = pl.ds(at, ROW_BLOCK)
        slopes = slopes_of(twice_ref[rows, :], col_pair, mat_ref[rows, pl.ds(first_col, width)])
        term = jnp.dot(turned_ref[:, rows], slopes, preferred_element_type=F32)
        total = term if total is None else total + term
    return (total[:rank] + total[rank:]).T


def first_kernel(
    outer_ref, high_ref, row_hbm, col_hbm, mat_hbm, twice_ref, pair_ref, turned_ref, one_ref, two_ref,
    row_ref, col_ref, mat_ref, sems,
):
    del outer_ref, high_ref
    width = col_ref.shape[0]
    loads = [
        pltpu.make_async_copy(row_hbm, row_ref, sems.at[0]),
        pltpu.make_async_copy(mat_hbm.at[:, pl.ds(0, width)], mat_ref, sems.at[1]),
        pltpu.make_async_copy(col_hbm.at[pl.ds(0, width), :], col_ref, sems.at[2]),
    ]
    for load in loads:
        load.start()
    loads[0].wait()
    high, low = split(row_ref[...])
    twice_ref[...] = jnp.concatenate([high, high], axis=1)
    pair_ref[...] = jnp.concatenate([high, low], axis=1)
    turned_ref[...] = jnp.concatenate([high.T, low.T], axis=0)
    loads[1].wait()
    loads[2].wait()
    out = col_partial(twice_ref, turned_ref, col_ref[...], mat_ref, 0)
    one_ref[...] = out[: one_ref.shape[0]]
    two_ref[...] = out[one_ref.shape[0] :]


def third_kernel(
    at, token_ref, col_hbm, mat_hbm, twice_ref, turned_ref, col_ref, mat_ref, out_ref, sems
):
    del token_ref
    width, columns = out_ref.shape[0], mat_ref.shape[1]
    soon = at + width
    loads = [
        pltpu.make_async_copy(mat_hbm.at[:, pl.ds(0, soon)], mat_ref.at[:, pl.ds(0, soon)], sems.at[0]),
        pltpu.make_async_copy(col_hbm, col_ref, sems.at[1]),
    ]
    if soon < columns:
        rest = pl.ds(soon, columns - soon)
        loads.append(pltpu.make_async_copy(mat_hbm.at[:, rest], mat_ref.at[:, rest], sems.at[2]))
    for load in loads:
        load.start()
    loads[0].wait()
    loads[1].wait()
    col = col_ref[pl.ds(at, width), :]
    out_ref[...] = col_partial(twice_ref, turned_ref, col, mat_ref, at)
    for load in loads[2:]:
        load.wait()


def pick(outer_ref, far_ref, near_ref):
    near = near_ref[...]
    return jnp.where(outer_ref[0] == 1, far_ref[: near.shape[0], :], near)


def pick_kernel(outer_ref, token_ref, far_ref, near_ref, out_ref):
    del token_ref
    out_ref[...] = pick(outer_ref, far_ref, near_ref)


def fresh_kernel(at, token_ref, twice_ref, turned_ref, col_ref, mat_ref, out_ref):
    del token_ref
    width = out_ref.shape[0]
    col = col_ref[pl.ds(at, width), :]
    out_ref[...] = col_partial(twice_ref, turned_ref, col, mat_ref, at)


def middle_kernel(
    at, rows_total, token_ref, outer_ref, far_ref, near_ref, twice_ref, turned_ref, mat_ref, col_ref, mean_ref,
    square_ref, new_ref, new_mean_ref, new_square_ref, out_ref,
):
    del token_ref
    total = pick(outer_ref, far_ref, near_ref)
    own = pl.ds(at, out_ref.shape[0])
    new, new_mean_ref[...], new_square_ref[...] = adam_move(
        col_ref[own, :], total / rows_total, mean_ref[own, :], square_ref[own, :], START + 1
    )
    new_ref[...] = new
    out_ref[...] = col_partial(twice_ref, turned_ref, new, mat_ref, at)


def last_kernel(at, rows_total, count, token_ref, outer_ref, pair_ref, mat_ref, *refs):
    del token_ref
    out_ref, grad_ref, news = refs[-1], refs[5 * count : -1 - count], []
    for index in range(count):
        far_ref, near_ref, col_ref, mean_ref, square_ref = refs[5 * index : 5 * index + 5]
        gradient = pick(outer_ref, far_ref, near_ref) / rows_total
        new, _, _ = adam_move(col_ref[...], gradient, mean_ref[...], square_ref[...], START + 2)
        refs[index - 1 - count][...] = new
        news.append(new)
    high, low = split(jnp.concatenate(news, axis=0))
    twice = jnp.concatenate([high, high], axis=1)
    pair = jnp.concatenate([high, low], axis=1)
    width, rank = high.shape
    for at_row in range(0, mat_ref.shape[0], ROW_BLOCK):
        rows = pl.ds(at_row, ROW_BLOCK)
        slopes = slopes_of(pair_ref[rows, :], twice, mat_ref[rows, pl.ds(at, width)])
        term = jnp.dot(slopes, pair, preferred_element_type=F32)
        term = term[:, :rank] + term[:, rank:]
        out_ref[rows, :] = grad_ref[0][rows, :] + term if grad_ref else term


def store_kernel(token_ref, *refs):
    del token_ref
    *chunk_refs, out_hbm, done_ref, sems = refs
    done_ref[...] = jnp.zeros_like(done_ref)
    stores, at = [], 0
    for index, chunk_ref in enumerate(chunk_refs):
        target = out_hbm.at[pl.ds(at, chunk_ref.shape[0]), :]
        stores.append(pltpu.make_async_copy(chunk_ref, target, sems.at[index]))
        at += chunk_ref.shape[0]
    for store in stores:
        store.start()
    for store in stores:
        store.wait()


def halves_kernel(high_ref, grad_ref, keep_ref, send_ref):
    half = keep_ref.shape[0]
    keep_ref[...] = grad_ref[pl.ds(pl.multiple_of(high_ref[0] * half, half), half), :]
    send_ref[...] = grad_ref[pl.ds(pl.multiple_of((1 - high_ref[0]) * half, half), half), :]


def row_kernel(cols_total, token_ref, high_ref, part_ref, other_ref, row_ref, mean_ref, square_ref, new_ref):
    del token_ref
    half = part_ref.shape[0]
    own = pl.ds(pl.multiple_of(high_ref[0] * half, half), half)
    gradient = (part_ref[...] + other_ref[...]) / cols_total
    new_ref[...], _, _ = adam_move(row_ref[own, :], gradient, mean_ref[own, :], square_ref[own, :], START + 1)


def join_kernel(high_ref, new_ref, other_ref, out_hbm, sems):
    half = new_ref.shape[0]
    own = pl.multiple_of(high_ref[0] * half, half)
    far = pl.multiple_of((1 - high_ref[0]) * half, half)
    stores = [
        pltpu.make_async_copy(new_ref, out_hbm.at[pl.ds(own, half), :], sems.at[0]),
        pltpu.make_async_copy(other_ref, out_hbm.at[pl.ds(far, half), :], sems.at[1]),
    ]
    for store in stores:
        store.start()
    for store in stores:
        store.wait()


VMEM = pl.BlockSpec(memory_space=pltpu.VMEM)
SMEM = pl.BlockSpec(memory_space=pltpu.SMEM)
ANY = pl.BlockSpec(memory_space=pl.ANY)
HBM = pl.BlockSpec(memory_space=pltpu.HBM)


def call(kernel, name, ins, outs, scratch=(), aliases=None):
    return pl.pallas_call(
        kernel,
        out_shape=[jax.ShapeDtypeStruct(shape, kind) for _, shape, kind in outs],
        in_specs=[spec for spec, _ in ins],
        out_specs=[spec for spec, _, _ in outs],
        scratch_shapes=scratch,
        input_output_aliases=aliases or {},
        compiler_params=pltpu.CompilerParams(vmem_limit_bytes=6 << 20),
        cost_estimate=pl.CostEstimate(flops=1, bytes_accessed=1, transcendentals=0),
        name=name,
    )(*[pltpu.with_memory_space_constraint(array, pltpu.HBM) if spec is HBM else array for spec, array in ins])


def chunks_of(columns):
    widths = [TARGET] * (columns // TARGET)
    if columns % TARGET:
        widths.append(columns % TARGET)
    return [(sum(widths[:index]), width) for index, width in enumerate(widths)]


class Work:
    def __init__(self, outer, high, matrix, row_factor, col_factor, col_mean, col_square, rows_total):
        self.outer, self.high, self.rows_total = outer, high, rows_total
        self.matrix, self.row = matrix, row_factor
        self.state = [col_factor, col_mean, col_square]
        self.rank = col_factor.shape[1]
        self.chunks = chunks_of(col_factor.shape[0])
        self.moved = {}
        self.new = {}
        self.grad = None

    def chunk(self, index):
        return (VMEM, (self.chunks[index][1], self.rank), F32)

    def first(self):
        rows, rank = self.row.shape
        width = sum(self.chunks[1])
        wide = (VMEM, (rows, 2 * rank), BF16)
        self.twice, self.pair, self.turned, out, self.early = call(
            first_kernel, "first",
            [(SMEM, self.outer), (SMEM, self.high), (HBM, self.row), (HBM, self.state[0]), (HBM, self.matrix)],
            [wide, wide, (VMEM, (2 * rank, rows), BF16), self.chunk(0), self.chunk(1)],
            scratch=[
                pltpu.VMEM(self.row.shape, F32),
                pltpu.VMEM((width, rank), F32),
                pltpu.VMEM((rows, width), BF16),
                pltpu.SemaphoreType.DMA((3,)),
            ],
        )
        return out

    def third(self, token):
        col = self.state[0]
        self.state[0], self.matrix, out = call(
            functools.partial(third_kernel, self.chunks[2][0]), "third",
            [(ANY, token), (HBM, col), (HBM, self.matrix), (VMEM, self.twice), (VMEM, self.turned)],
            [(VMEM, col.shape, F32), (VMEM, self.matrix.shape, BF16), self.chunk(2)],
            scratch=[pltpu.SemaphoreType.DMA((3,))],
        )
        return out

    def fresh(self, index, token):
        if index == 1:
            return self.early
        if index == 2:
            return self.third(token)
        (out,) = call(
            functools.partial(fresh_kernel, self.chunks[index][0]), "fresh",
            [(ANY, token), (VMEM, self.twice), (VMEM, self.turned), (VMEM, self.state[0]), (VMEM, self.matrix)],
            [self.chunk(index)],
        )
        return out

    def middle(self, index, far, near, token):
        *self.moved[index], out = call(
            functools.partial(middle_kernel, self.chunks[index][0], self.rows_total), "middle",
            [(ANY, token), (SMEM, self.outer), (VMEM, far), (VMEM, near), (VMEM, self.twice), (VMEM, self.turned)]
            + [(VMEM, array) for array in (self.matrix, *self.state)],
            [self.chunk(index)] * 4,
        )
        return out

    def last(self, indices, far, near, token):
        ins = [(ANY, token), (SMEM, self.outer), (VMEM, self.pair), (VMEM, self.matrix)]
        for index in indices:
            ins += [(VMEM, array) for array in (far[index], near[index], *self.moved[index])]
        aliases = None
        if self.grad is not None:
            aliases = {len(ins): len(indices)}
            ins.append((VMEM, self.grad))
        *new, self.grad = call(
            functools.partial(last_kernel, self.chunks[indices[0]][0], self.rows_total, len(indices)), "last",
            ins,
            [*map(self.chunk, indices), (VMEM, self.row.shape, F32)],
            aliases=aliases,
        )
        self.new.update(zip(indices, new, strict=True))

    def new_cols(self, token):
        return call(
            store_kernel, "store",
            [(ANY, token)] + [(VMEM, self.new[index]) for index in range(len(self.chunks))],
            [(HBM, self.state[0].shape, F32), (VMEM, (8, self.rank), F32)],
            scratch=[pltpu.SemaphoreType.DMA((len(self.chunks),))],
        )


def plain_columns(work):
    every = range(len(work.chunks))
    sums = [lax.psum(work.first(), "row")]
    for index in every[1:]:
        sums.append(lax.psum(work.fresh(index, sums[0]), "row"))
    sums = [lax.psum(work.middle(index, sums[index], sums[index], sums[index]), "row") for index in every]
    for index in every:
        work.last([index], sums, sums, sums[index])


def join_sums_kernel(token_ref, own_ref, arrived_ref, out_ref):
    del token_ref
    out_ref[...] = own_ref[...] + arrived_ref[: out_ref.shape[0], :]


def merge_kernel(which, outer_ref, token_ref, *refs):
    del token_ref
    refs = dict(zip(which, refs, strict=True))
    outer = outer_ref[0] == 1
    if "whole" in refs:
        whole = refs["joined"][...] + refs["from_inner"][...]
        refs["whole"][...] = whole
        if "payload" in refs:
            own = refs["own"][...]
            low, high = sorted((own.shape[0], whole.shape[0]))
            refs["payload"][:low, :] = jnp.where(outer, own[:low], whole[:low])
            if high > low:
                refs["payload"][low:, :] = own[low:] if own.shape[0] == high else whole[low:]
    elif "payload" in refs:
        refs["payload"][...] = refs["own"][...]


def line_columns(work):
    n_col = lax.axis_size("col")
    outer_pairs = [(0, 1), (1, 0), (2, 3), (3, 2)]
    inner_pairs = []
    for col in range(n_col):
        inner_pairs += [(n_col + col, 2 * n_col + col), (2 * n_col + col, n_col + col)]
        inner_pairs += [(at * n_col + col, at * n_col + (col ^ 1)) for at in (0, 3)]
    chunks = len(work.chunks)
    slots = 2 * chunks
    own, joined, whole, from_outer, from_inner = {}, {}, {}, {}, {}
    far, near, pending = {}, {}, []
    own[0] = work.first()
    token = own[0]
    for k in range(slots + 2 * OUTER_LAG + INNER_LAG):
        here = k - OUTER_LAG
        then = here - INNER_LAG
        done = then - OUTER_LAG
        if 0 <= here < slots:
            (joined[here],) = call(
                join_sums_kernel, "sum",
                [(ANY, token), (VMEM, own[here]), (VMEM, from_outer[here])],
                [work.chunk(here % chunks)],
            )
            token = joined[here]
            from_inner[k] = lax.ppermute(joined[here], ("row", "col"), inner_pairs)
        ins, outs = {}, {}
        if 0 <= then < slots:
            ins["joined"], ins["from_inner"] = joined[then], from_inner[k - INNER_LAG]
            outs["whole"] = work.chunk(then % chunks)
            if k < slots:
                ins["own"] = own[k]
                outs["payload"] = max(work.chunk(then % chunks), work.chunk(k % chunks), key=lambda o: o[1])
        if k < OUTER_LAG + INNER_LAG:
            ins["own"], outs["payload"] = own[k], work.chunk(k)
        if outs:
            got = call(
                functools.partial(merge_kernel, [*ins, *outs]), "merge",
                [(SMEM, work.outer), (ANY, token)] + [(VMEM, array) for array in ins.values()],
                [*outs.values()],
            )
            got = dict(zip(outs, got, strict=True))
            token = got[[*outs][-1]]
            if "whole" in got:
                whole[then] = got["whole"]
        if k < slots + OUTER_LAG + INNER_LAG:
            payload = got["payload"] if k < slots else whole[then]
            from_outer[k] = lax.ppermute(payload, "row", outer_pairs)
        early = k - 2 * OUTER_LAG - INNER_LAG + 1
        if k >= slots + INNER_LAG and early < slots:
            at = early - chunks
            (token,) = call(
                pick_kernel, "pick",
                [(SMEM, work.outer), (ANY, token), (VMEM, from_outer[k - OUTER_LAG + 1]), (VMEM, whole[early])],
                [work.chunk(at)],
            )
            far[at] = near[at] = token
            pending.append(at)
        nxt = k + 1
        if nxt < chunks:
            token = own[nxt] = work.fresh(nxt, token)
        elif nxt < slots:
            at = nxt - chunks
            token = own[nxt] = work.middle(at, from_outer[at + OUTER_LAG + INNER_LAG], whole[at], token)
        at = done - chunks
        if at >= 0 and at not in far:
            far[at], near[at] = from_outer[done + OUTER_LAG + INNER_LAG], whole[done]
            pending.append(at)
        pending.sort()
        if pending and nxt >= slots:
            count = BATCH if done + 1 < slots else len(pending)
            batch, pending = pending[:count], pending[count:]
            work.last(batch, far, near, token)
            token = work.grad


def row_step(work, row_mean, row_square, cols_total):
    high, grad = work.high, work.grad
    rows, rank = grad.shape
    half = (VMEM, (rows // 2, rank), F32)
    swap = [(0, 1), (1, 0), (2, 3), (3, 2)]
    across = [(0, 2), (2, 0), (1, 3), (3, 1)]
    keep, send = call(halves_kernel, "halves", [(SMEM, high), (VMEM, grad)], [half, half])
    part = keep + lax.ppermute(send, "col", swap)
    other = lax.ppermute(part, "col", across)
    new_cols, stored = work.new_cols(part)
    ins = [(VMEM, array) for array in (part, other, work.row, row_mean, row_square)]
    (new,) = call(
        functools.partial(row_kernel, cols_total), "row", [(ANY, stored), (SMEM, high), *ins], [half]
    )
    other = lax.ppermute(new, "col", swap)
    (out,) = call(
        join_kernel, "join",
        [(SMEM, high), (VMEM, new), (VMEM, other)],
        [(HBM, grad.shape, F32)],
        scratch=[pltpu.SemaphoreType.DMA((2,))],
    )
    return out, new_cols


def on_device(matrix, row_factor, col_factor, row_mean, row_square, col_mean, col_square):
    n_row = lax.axis_size("row")
    n_col = lax.axis_size("col")
    row, col = lax.axis_index("row"), lax.axis_index("col")
    outer = ((row == 0) | (row == n_row - 1)).astype(jnp.int32).reshape(1)
    high = (col & 1).astype(jnp.int32).reshape(1)
    work = Work(outer, high, matrix, row_factor, col_factor, col_mean, col_square, matrix.shape[0] * n_row)
    if n_row == 4 and n_col % 2 == 0:
        line_columns(work)
    else:
        plain_columns(work)
    cols_total = matrix.shape[1] * n_col
    if n_col == 4:
        new_rows, new_cols = row_step(work, row_mean, row_square, cols_total)
    else:
        new_cols, _ = work.new_cols(work.grad)
        summed = lax.psum(work.grad, "col")
        new_rows, _, _ = adam_move(row_factor, summed / cols_total, row_mean, row_square, START + 1)
    return new_rows, new_cols


def solution(mesh):
    return jax.shard_map(
        on_device,
        mesh=mesh,
        in_specs=(
            P(("grp", "row"), "col"),
            P(("grp", "row"), None),
            P(("grp", "col"), None),
            P(("grp", "row"), None),
            P(("grp", "row"), None),
            P(("grp", "col"), None),
            P(("grp", "col"), None),
        ),
        out_specs=(P(("grp", "row"), None), P(("grp", "col"), None)),
        check_vma=False,
    )
```

```python
import functools

import jax
import jax.numpy as jnp
from jax import lax
from jax.experimental import pallas as pl
from jax.experimental.pallas import tpu as pltpu
from jax.sharding import PartitionSpec as P

START = 100
DELTA = 1.0
LEARN_RATE = 0.05
BETA_ONE = 0.9
BETA_TWO = 0.999
EPSILON = 1e-08
F32, BF16 = jnp.float32, jnp.bfloat16
NT = (((1,), (1,)), ((), ()))
ROW_BLOCK = 1024
UNIT = 128
TARGET = 256
OUTER_LAG = 3
INNER_LAG = 2
BATCH = 3


def adam_move(values, gradient, first_moment, square, counter):
    first_moment = BETA_ONE * first_moment + (1.0 - BETA_ONE) * gradient
    square = BETA_TWO * square + (1.0 - BETA_TWO) * gradient * gradient
    fixed_mean = first_moment / (1.0 - BETA_ONE**counter)
    fixed_square = square / (1.0 - BETA_TWO**counter)
    return (
        values - LEARN_RATE * fixed_mean / (jnp.sqrt(fixed_square) + EPSILON),
        first_moment,
        square,
    )


def split(values):
    high = values.astype(BF16)
    return high, (values - high.astype(F32)).astype(BF16)


def slopes_of(row_pair, col_pair, block):
    fitted = lax.dot_general(row_pair, col_pair, NT, preferred_element_type=F32)
    return jnp.clip(fitted - block.astype(F32), -DELTA, DELTA).astype(BF16)


def col_partial(twice_ref, turned_ref, col, mat_ref, first_col):
    col_pair = jnp.concatenate(split(col), axis=1)
    width, rank = col.shape
    total = None
    for at in range(0, mat_ref.shape[0], ROW_BLOCK):
        rows = pl.ds(at, ROW_BLOCK)
        slopes = slopes_of(twice_ref[rows, :], col_pair, mat_ref[rows, pl.ds(first_col, width)])
        term = jnp.dot(turned_ref[:, rows], slopes, preferred_element_type=F32)
        total = term if total is None else total + term
    return (total[:rank] + total[rank:]).T


def first_kernel(
    outer_ref, high_ref, row_hbm, col_hbm, mat_hbm, twice_ref, pair_ref, turned_ref, one_ref, two_ref,
    row_ref, col_ref, mat_ref, sems,
):
    del outer_ref, high_ref
    width = col_ref.shape[0]
    loads = [
        pltpu.make_async_copy(row_hbm, row_ref, sems.at[0]),
        pltpu.make_async_copy(mat_hbm.at[:, pl.ds(0, width)], mat_ref, sems.at[1]),
        pltpu.make_async_copy(col_hbm.at[pl.ds(0, width), :], col_ref, sems.at[2]),
    ]
    for load in loads:
        load.start()
    loads[0].wait()
    high, low = split(row_ref[...])
    twice_ref[...] = jnp.concatenate([high, high], axis=1)
    pair_ref[...] = jnp.concatenate([high, low], axis=1)
    turned_ref[...] = jnp.concatenate([high.T, low.T], axis=0)
    loads[1].wait()
    loads[2].wait()
    out = col_partial(twice_ref, turned_ref, col_ref[...], mat_ref, 0)
    one_ref[...] = out[: one_ref.shape[0]]
    two_ref[...] = out[one_ref.shape[0] :]


def third_kernel(
    at, token_ref, col_hbm, mat_hbm, twice_ref, turned_ref, col_ref, mat_ref, out_ref, sems
):
    del token_ref
    width, columns = out_ref.shape[0], mat_ref.shape[1]
    soon = at + width
    loads = [
        pltpu.make_async_copy(mat_hbm.at[:, pl.ds(0, soon)], mat_ref.at[:, pl.ds(0, soon)], sems.at[0]),
        pltpu.make_async_copy(col_hbm, col_ref, sems.at[1]),
    ]
    if soon < columns:
        rest = pl.ds(soon, columns - soon)
        loads.append(pltpu.make_async_copy(mat_hbm.at[:, rest], mat_ref.at[:, rest], sems.at[2]))
    for load in loads:
        load.start()
    loads[0].wait()
    loads[1].wait()
    col = col_ref[pl.ds(at, width), :]
    out_ref[...] = col_partial(twice_ref, turned_ref, col, mat_ref, at)
    for load in loads[2:]:
        load.wait()


def pick(outer_ref, far_ref, near_ref):
    near = near_ref[...]
    return jnp.where(outer_ref[0] == 1, far_ref[: near.shape[0], :], near)


def pick_kernel(outer_ref, token_ref, far_ref, near_ref, out_ref):
    del token_ref
    out_ref[...] = pick(outer_ref, far_ref, near_ref)


def fresh_kernel(at, token_ref, twice_ref, turned_ref, col_ref, mat_ref, out_ref):
    del token_ref
    width = out_ref.shape[0]
    col = col_ref[pl.ds(at, width), :]
    out_ref[...] = col_partial(twice_ref, turned_ref, col, mat_ref, at)


def middle_kernel(
    at, rows_total, token_ref, outer_ref, far_ref, near_ref, twice_ref, turned_ref, mat_ref, col_ref, mean_ref,
    square_ref, new_ref, new_mean_ref, new_square_ref, out_ref,
):
    del token_ref
    total = pick(outer_ref, far_ref, near_ref)
    own = pl.ds(at, out_ref.shape[0])
    new, new_mean_ref[...], new_square_ref[...] = adam_move(
        col_ref[own, :], total / rows_total, mean_ref[own, :], square_ref[own, :], START + 1
    )
    new_ref[...] = new
    out_ref[...] = col_partial(twice_ref, turned_ref, new, mat_ref, at)


def last_kernel(at, rows_total, count, token_ref, outer_ref, pair_ref, mat_ref, *refs):
    del token_ref
    out_ref, grad_ref, news = refs[-1], refs[5 * count : -1 - count], []
    for index in range(count):
        far_ref, near_ref, col_ref, mean_ref, square_ref = refs[5 * index : 5 * index + 5]
        gradient = pick(outer_ref, far_ref, near_ref) / rows_total
        new, _, _ = adam_move(col_ref[...], gradient, mean_ref[...], square_ref[...], START + 2)
        refs[index - 1 - count][...] = new
        news.append(new)
    high, low = split(jnp.concatenate(news, axis=0))
    twice = jnp.concatenate([high, high], axis=1)
    pair = jnp.concatenate([high, low], axis=1)
    width, rank = high.shape
    for at_row in range(0, mat_ref.shape[0], ROW_BLOCK):
        rows = pl.ds(at_row, ROW_BLOCK)
        slopes = slopes_of(pair_ref[rows, :], twice, mat_ref[rows, pl.ds(at, width)])
        term = jnp.dot(slopes, pair, preferred_element_type=F32)
        term = term[:, :rank] + term[:, rank:]
        out_ref[rows, :] = grad_ref[0][rows, :] + term if grad_ref else term


def store_kernel(token_ref, *refs):
    del token_ref
    *chunk_refs, out_hbm, done_ref, sems = refs
    done_ref[...] = jnp.zeros_like(done_ref)
    stores, at = [], 0
    for index, chunk_ref in enumerate(chunk_refs):
        target = out_hbm.at[pl.ds(at, chunk_ref.shape[0]), :]
        stores.append(pltpu.make_async_copy(chunk_ref, target, sems.at[index]))
        at += chunk_ref.shape[0]
    for store in stores:
        store.start()
    for store in stores:
        store.wait()


def half_share(start, at, width, pair_ref, new, mat_ref, grad_ref, out_ref):
    high, low = split(new)
    twice = jnp.concatenate([high, high], axis=1)
    pair = jnp.concatenate([high, low], axis=1)
    rank, half = new.shape[1], out_ref.shape[0]
    rows = pl.ds(pl.multiple_of(start * half, half), half)
    slopes = slopes_of(pair_ref[rows, :], twice, mat_ref[rows, pl.ds(at, width)])
    term = jnp.dot(slopes, pair, preferred_element_type=F32)
    out_ref[...] = grad_ref[rows, :] + term[:, :rank] + term[:, rank:]


def send_kernel(
    at, rows_total, token_ref, outer_ref, high_ref, pair_ref, mat_ref, far_ref, near_ref, col_ref, mean_ref,
    square_ref, grad_ref, new_ref, out_ref,
):
    del token_ref
    gradient = pick(outer_ref, far_ref, near_ref) / rows_total
    new, _, _ = adam_move(col_ref[...], gradient, mean_ref[...], square_ref[...], START + 2)
    new_ref[...] = new
    half_share(1 - high_ref[0], at, new.shape[0], pair_ref, new, mat_ref, grad_ref, out_ref)


def keep_kernel(at, token_ref, high_ref, pair_ref, mat_ref, new_ref, grad_ref, out_ref):
    del token_ref
    half_share(high_ref[0], at, new_ref.shape[0], pair_ref, new_ref[...], mat_ref, grad_ref, out_ref)


def row_kernel(cols_total, token_ref, high_ref, part_ref, other_ref, row_ref, mean_ref, square_ref, new_ref):
    del token_ref
    half = part_ref.shape[0]
    own = pl.ds(pl.multiple_of(high_ref[0] * half, half), half)
    gradient = (part_ref[...] + other_ref[...]) / cols_total
    new_ref[...], _, _ = adam_move(row_ref[own, :], gradient, mean_ref[own, :], square_ref[own, :], START + 1)


def join_kernel(high_ref, new_ref, other_ref, out_hbm, sems):
    half = new_ref.shape[0]
    own = pl.multiple_of(high_ref[0] * half, half)
    far = pl.multiple_of((1 - high_ref[0]) * half, half)
    stores = [
        pltpu.make_async_copy(new_ref, out_hbm.at[pl.ds(own, half), :], sems.at[0]),
        pltpu.make_async_copy(other_ref, out_hbm.at[pl.ds(far, half), :], sems.at[1]),
    ]
    for store in stores:
        store.start()
    for store in stores:
        store.wait()


VMEM = pl.BlockSpec(memory_space=pltpu.VMEM)
SMEM = pl.BlockSpec(memory_space=pltpu.SMEM)
ANY = pl.BlockSpec(memory_space=pl.ANY)
HBM = pl.BlockSpec(memory_space=pltpu.HBM)


def call(kernel, name, ins, outs, scratch=(), aliases=None):
    return pl.pallas_call(
        kernel,
        out_shape=[jax.ShapeDtypeStruct(shape, kind) for _, shape, kind in outs],
        in_specs=[spec for spec, _ in ins],
        out_specs=[spec for spec, _, _ in outs],
        scratch_shapes=scratch,
        input_output_aliases=aliases or {},
        compiler_params=pltpu.CompilerParams(vmem_limit_bytes=6 << 20),
        cost_estimate=pl.CostEstimate(flops=1, bytes_accessed=1, transcendentals=0),
        name=name,
    )(*[pltpu.with_memory_space_constraint(array, pltpu.HBM) if spec is HBM else array for spec, array in ins])


def chunks_of(columns):
    widths = [TARGET] * (columns // TARGET)
    if columns % TARGET:
        widths.append(columns % TARGET)
    return [(sum(widths[:index]), width) for index, width in enumerate(widths)]


class Work:
    def __init__(self, outer, high, halved, matrix, row_factor, col_factor, col_mean, col_square, rows_total):
        self.outer, self.high, self.rows_total = outer, high, rows_total
        self.matrix, self.row = matrix, row_factor
        self.state = [col_factor, col_mean, col_square]
        self.rank = col_factor.shape[1]
        self.chunks = chunks_of(col_factor.shape[0])
        self.moved = {}
        self.new = {}
        self.grad, self.halved = None, halved

    def chunk(self, index):
        return (VMEM, (self.chunks[index][1], self.rank), F32)

    def first(self):
        rows, rank = self.row.shape
        width = sum(self.chunks[1])
        wide = (VMEM, (rows, 2 * rank), BF16)
        self.twice, self.pair, self.turned, out, self.early = call(
            first_kernel, "first",
            [(SMEM, self.outer), (SMEM, self.high), (HBM, self.row), (HBM, self.state[0]), (HBM, self.matrix)],
            [wide, wide, (VMEM, (2 * rank, rows), BF16), self.chunk(0), self.chunk(1)],
            scratch=[
                pltpu.VMEM(self.row.shape, F32),
                pltpu.VMEM((width, rank), F32),
                pltpu.VMEM((rows, width), BF16),
                pltpu.SemaphoreType.DMA((3,)),
            ],
        )
        return out

    def third(self, token):
        col = self.state[0]
        self.state[0], self.matrix, out = call(
            functools.partial(third_kernel, self.chunks[2][0]), "third",
            [(ANY, token), (HBM, col), (HBM, self.matrix), (VMEM, self.twice), (VMEM, self.turned)],
            [(VMEM, col.shape, F32), (VMEM, self.matrix.shape, BF16), self.chunk(2)],
            scratch=[pltpu.SemaphoreType.DMA((3,))],
        )
        return out

    def fresh(self, index, token):
        if index == 1:
            return self.early
        if index == 2:
            return self.third(token)
        (out,) = call(
            functools.partial(fresh_kernel, self.chunks[index][0]), "fresh",
            [(ANY, token), (VMEM, self.twice), (VMEM, self.turned), (VMEM, self.state[0]), (VMEM, self.matrix)],
            [self.chunk(index)],
        )
        return out

    def middle(self, index, far, near, token):
        *self.moved[index], out = call(
            functools.partial(middle_kernel, self.chunks[index][0], self.rows_total), "middle",
            [(ANY, token), (SMEM, self.outer), (VMEM, far), (VMEM, near), (VMEM, self.twice), (VMEM, self.turned)]
            + [(VMEM, array) for array in (self.matrix, *self.state)],
            [self.chunk(index)] * 4,
        )
        return out

    def last(self, indices, far, near, token):
        final = len(self.chunks) - 1
        if self.halved and final in indices:
            if len(indices) > 1:
                self.last(indices[:-1], far, near, token)
                token = self.grad
            return self.halves(final, far[final], near[final], token)
        ins = [(ANY, token), (SMEM, self.outer), (VMEM, self.pair), (VMEM, self.matrix)]
        for index in indices:
            ins += [(VMEM, array) for array in (far[index], near[index], *self.moved[index])]
        aliases = None
        if self.grad is not None:
            aliases = {len(ins): len(indices)}
            ins.append((VMEM, self.grad))
        *new, self.grad = call(
            functools.partial(last_kernel, self.chunks[indices[0]][0], self.rows_total, len(indices)), "last",
            ins,
            [*map(self.chunk, indices), (VMEM, self.row.shape, F32)],
            aliases=aliases,
        )
        self.new.update(zip(indices, new, strict=True))

    def halves(self, index, far, near, token):
        at = self.chunks[index][0]
        rows, rank = self.row.shape
        half = (VMEM, (rows // 2, rank), F32)
        ins = [(VMEM, array) for array in (far, near, *self.moved[index], self.grad)]
        self.new[index], send = call(
            functools.partial(send_kernel, at, self.rows_total), "send",
            [(ANY, token), (SMEM, self.outer), (SMEM, self.high), (VMEM, self.pair), (VMEM, self.matrix), *ins],
            [self.chunk(index), half],
        )
        (keep,) = call(
            functools.partial(keep_kernel, at), "keep",
            [(ANY, send), (SMEM, self.high)]
            + [(VMEM, array) for array in (self.pair, self.matrix, self.new[index], self.grad)],
            [half],
        )
        self.ends = keep, send

    def new_cols(self, token):
        return call(
            store_kernel, "store",
            [(ANY, token)] + [(VMEM, self.new[index]) for index in range(len(self.chunks))],
            [(HBM, self.state[0].shape, F32), (VMEM, (8, self.rank), F32)],
            scratch=[pltpu.SemaphoreType.DMA((len(self.chunks),))],
        )


def plain_columns(work):
    every = range(len(work.chunks))
    sums = [lax.psum(work.first(), "row")]
    for index in every[1:]:
        sums.append(lax.psum(work.fresh(index, sums[0]), "row"))
    sums = [lax.psum(work.middle(index, sums[index], sums[index], sums[index]), "row") for index in every]
    for index in every:
        work.last([index], sums, sums, sums[index])


def join_sums_kernel(token_ref, own_ref, arrived_ref, out_ref):
    del token_ref
    out_ref[...] = own_ref[...] + arrived_ref[: out_ref.shape[0], :]


def merge_kernel(which, outer_ref, token_ref, *refs):
    del token_ref
    refs = dict(zip(which, refs, strict=True))
    outer = outer_ref[0] == 1
    if "whole" in refs:
        whole = refs["joined"][...] + refs["from_inner"][...]
        refs["whole"][...] = whole
        if "payload" in refs:
            own = refs["own"][...]
            low, high = sorted((own.shape[0], whole.shape[0]))
            refs["payload"][:low, :] = jnp.where(outer, own[:low], whole[:low])
            if high > low:
                refs["payload"][low:, :] = own[low:] if own.shape[0] == high else whole[low:]
    elif "payload" in refs:
        refs["payload"][...] = refs["own"][...]


def line_columns(work):
    n_col = lax.axis_size("col")
    outer_pairs = [(0, 1), (1, 0), (2, 3), (3, 2)]
    inner_pairs = []
    for col in range(n_col):
        inner_pairs += [(n_col + col, 2 * n_col + col), (2 * n_col + col, n_col + col)]
        inner_pairs += [(at * n_col + col, at * n_col + (col ^ 1)) for at in (0, 3)]
    chunks = len(work.chunks)
    slots = 2 * chunks
    own, joined, whole, from_outer, from_inner = {}, {}, {}, {}, {}
    far, near, pending = {}, {}, []
    own[0] = work.first()
    token = own[0]
    for k in range(slots + 2 * OUTER_LAG + INNER_LAG):
        here = k - OUTER_LAG
        then = here - INNER_LAG
        done = then - OUTER_LAG
        if 0 <= here < slots:
            (joined[here],) = call(
                join_sums_kernel, "sum",
                [(ANY, token), (VMEM, own[here]), (VMEM, from_outer[here])],
                [work.chunk(here % chunks)],
            )
            token = joined[here]
            from_inner[k] = lax.ppermute(joined[here], ("row", "col"), inner_pairs)
        ins, outs = {}, {}
        if 0 <= then < slots:
            ins["joined"], ins["from_inner"] = joined[then], from_inner[k - INNER_LAG]
            outs["whole"] = work.chunk(then % chunks)
            if k < slots:
                ins["own"] = own[k]
                outs["payload"] = max(work.chunk(then % chunks), work.chunk(k % chunks), key=lambda o: o[1])
        if k < OUTER_LAG + INNER_LAG:
            ins["own"], outs["payload"] = own[k], work.chunk(k)
        if outs:
            got = call(
                functools.partial(merge_kernel, [*ins, *outs]), "merge",
                [(SMEM, work.outer), (ANY, token)] + [(VMEM, array) for array in ins.values()],
                [*outs.values()],
            )
            got = dict(zip(outs, got, strict=True))
            token = got[[*outs][-1]]
            if "whole" in got:
                whole[then] = got["whole"]
        if k < slots + OUTER_LAG + INNER_LAG:
            payload = got["payload"] if k < slots else whole[then]
            from_outer[k] = lax.ppermute(payload, "row", outer_pairs)
        early = k - 2 * OUTER_LAG - INNER_LAG + 1
        if k >= slots + INNER_LAG and early < slots:
            at = early - chunks
            (token,) = call(
                pick_kernel, "pick",
                [(SMEM, work.outer), (ANY, token), (VMEM, from_outer[k - OUTER_LAG + 1]), (VMEM, whole[early])],
                [work.chunk(at)],
            )
            far[at] = near[at] = token
            pending.append(at)
        nxt = k + 1
        if nxt < chunks:
            token = own[nxt] = work.fresh(nxt, token)
        elif nxt < slots:
            at = nxt - chunks
            token = own[nxt] = work.middle(at, from_outer[at + OUTER_LAG + INNER_LAG], whole[at], token)
        at = done - chunks
        if at >= 0 and at not in far:
            far[at], near[at] = from_outer[done + OUTER_LAG + INNER_LAG], whole[done]
            pending.append(at)
        pending.sort()
        if pending and nxt >= slots:
            count = BATCH if done + 1 < slots else len(pending)
            batch, pending = pending[:count], pending[count:]
            work.last(batch, far, near, token)
            token = work.grad


def row_step(work, row_mean, row_square, cols_total):
    high = work.high
    rows, rank = work.row.shape
    half = (VMEM, (rows // 2, rank), F32)
    swap = [(0, 1), (1, 0), (2, 3), (3, 2)]
    across = [(0, 2), (2, 0), (1, 3), (3, 1)]
    keep, send = work.ends
    part = keep + lax.ppermute(send, "col", swap)
    other = lax.ppermute(part, "col", across)
    new_cols, stored = work.new_cols(part)
    ins = [(VMEM, array) for array in (part, other, work.row, row_mean, row_square)]
    (new,) = call(
        functools.partial(row_kernel, cols_total), "row", [(ANY, stored), (SMEM, high), *ins], [half]
    )
    other = lax.ppermute(new, "col", swap)
    (out,) = call(
        join_kernel, "join",
        [(SMEM, high), (VMEM, new), (VMEM, other)],
        [(HBM, work.row.shape, F32)],
        scratch=[pltpu.SemaphoreType.DMA((2,))],
    )
    return out, new_cols


def on_device(matrix, row_factor, col_factor, row_mean, row_square, col_mean, col_square):
    n_row = lax.axis_size("row")
    n_col = lax.axis_size("col")
    row, col = lax.axis_index("row"), lax.axis_index("col")
    outer = ((row == 0) | (row == n_row - 1)).astype(jnp.int32).reshape(1)
    high = (col & 1).astype(jnp.int32).reshape(1)
    work = Work(outer, high, n_col == 4, matrix, row_factor, col_factor, col_mean, col_square, matrix.shape[0] * n_row)
    if n_row == 4 and n_col % 2 == 0:
        line_columns(work)
    else:
        plain_columns(work)
    cols_total = matrix.shape[1] * n_col
    if n_col == 4:
        new_rows, new_cols = row_step(work, row_mean, row_square, cols_total)
    else:
        new_cols, _ = work.new_cols(work.grad)
        summed = lax.psum(work.grad, "col")
        new_rows, _, _ = adam_move(row_factor, summed / cols_total, row_mean, row_square, START + 1)
    return new_rows, new_cols


def solution(mesh):
    return jax.shard_map(
        on_device,
        mesh=mesh,
        in_specs=(
            P(("grp", "row"), "col"),
            P(("grp", "row"), None),
            P(("grp", "col"), None),
            P(("grp", "row"), None),
            P(("grp", "row"), None),
            P(("grp", "col"), None),
            P(("grp", "col"), None),
        ),
        out_specs=(P(("grp", "row"), None), P(("grp", "col"), None)),
        check_vma=False,
    )
```

```python
import functools

import jax
import jax.numpy as jnp
from jax import lax
from jax.experimental import pallas as pl
from jax.experimental.pallas import tpu as pltpu
from jax.sharding import PartitionSpec as P

START = 100
DELTA = 1.0
LEARN_RATE = 0.05
BETA_ONE = 0.9
BETA_TWO = 0.999
EPSILON = 1e-08
F32, BF16 = jnp.float32, jnp.bfloat16
NT = (((1,), (1,)), ((), ()))
ROW_BLOCK = 1024
UNIT = 128
TARGET = 256
OUTER_LAG = 3
INNER_LAG = 2
BATCH = 3
PIECES = 2


def adam_move(values, gradient, first_moment, square, counter):
    first_moment = BETA_ONE * first_moment + (1.0 - BETA_ONE) * gradient
    square = BETA_TWO * square + (1.0 - BETA_TWO) * gradient * gradient
    fixed_mean = first_moment / (1.0 - BETA_ONE**counter)
    fixed_square = square / (1.0 - BETA_TWO**counter)
    return (
        values - LEARN_RATE * fixed_mean / (jnp.sqrt(fixed_square) + EPSILON),
        first_moment,
        square,
    )


def split(values):
    high = values.astype(BF16)
    return high, (values - high.astype(F32)).astype(BF16)


def slopes_of(row_pair, col_pair, block):
    fitted = lax.dot_general(row_pair, col_pair, NT, preferred_element_type=F32)
    return jnp.clip(fitted - block.astype(F32), -DELTA, DELTA).astype(BF16)


def col_partial(twice_ref, turned_ref, col, mat_ref, first_col):
    col_pair = jnp.concatenate(split(col), axis=1)
    width, rank = col.shape
    total = None
    for at in range(0, mat_ref.shape[0], ROW_BLOCK):
        rows = pl.ds(at, ROW_BLOCK)
        slopes = slopes_of(twice_ref[rows, :], col_pair, mat_ref[rows, pl.ds(first_col, width)])
        term = jnp.dot(turned_ref[:, rows], slopes, preferred_element_type=F32)
        total = term if total is None else total + term
    return (total[:rank] + total[rank:]).T


def first_kernel(
    outer_ref, high_ref, row_hbm, col_hbm, mat_hbm, twice_ref, pair_ref, turned_ref, one_ref, two_ref,
    row_ref, col_ref, mat_ref, sems,
):
    del outer_ref, high_ref
    width = col_ref.shape[0]
    loads = [
        pltpu.make_async_copy(row_hbm, row_ref, sems.at[0]),
        pltpu.make_async_copy(mat_hbm.at[:, pl.ds(0, width)], mat_ref, sems.at[1]),
        pltpu.make_async_copy(col_hbm.at[pl.ds(0, width), :], col_ref, sems.at[2]),
    ]
    for load in loads:
        load.start()
    loads[0].wait()
    high, low = split(row_ref[...])
    twice_ref[...] = jnp.concatenate([high, high], axis=1)
    pair_ref[...] = jnp.concatenate([high, low], axis=1)
    turned_ref[...] = jnp.concatenate([high.T, low.T], axis=0)
    loads[1].wait()
    loads[2].wait()
    out = col_partial(twice_ref, turned_ref, col_ref[...], mat_ref, 0)
    one_ref[...] = out[: one_ref.shape[0]]
    two_ref[...] = out[one_ref.shape[0] :]


def third_kernel(
    at, token_ref, col_hbm, mat_hbm, twice_ref, turned_ref, col_ref, mat_ref, out_ref, sems
):
    del token_ref
    width, columns = out_ref.shape[0], mat_ref.shape[1]
    soon = at + width
    loads = [
        pltpu.make_async_copy(mat_hbm.at[:, pl.ds(0, soon)], mat_ref.at[:, pl.ds(0, soon)], sems.at[0]),
        pltpu.make_async_copy(col_hbm, col_ref, sems.at[1]),
    ]
    if soon < columns:
        rest = pl.ds(soon, columns - soon)
        loads.append(pltpu.make_async_copy(mat_hbm.at[:, rest], mat_ref.at[:, rest], sems.at[2]))
    for load in loads:
        load.start()
    loads[0].wait()
    loads[1].wait()
    col = col_ref[pl.ds(at, width), :]
    out_ref[...] = col_partial(twice_ref, turned_ref, col, mat_ref, at)
    for load in loads[2:]:
        load.wait()


def pick(outer_ref, far_ref, near_ref):
    near = near_ref[...]
    return jnp.where(outer_ref[0] == 1, far_ref[: near.shape[0], :], near)


def pick_kernel(outer_ref, token_ref, far_ref, near_ref, out_ref):
    del token_ref
    out_ref[...] = pick(outer_ref, far_ref, near_ref)


def fresh_kernel(at, token_ref, twice_ref, turned_ref, col_ref, mat_ref, out_ref):
    del token_ref
    width = out_ref.shape[0]
    col = col_ref[pl.ds(at, width), :]
    out_ref[...] = col_partial(twice_ref, turned_ref, col, mat_ref, at)


def middle_kernel(
    at, rows_total, token_ref, outer_ref, far_ref, near_ref, twice_ref, turned_ref, mat_ref, col_ref, mean_ref,
    square_ref, new_ref, new_mean_ref, new_square_ref, out_ref,
):
    del token_ref
    total = pick(outer_ref, far_ref, near_ref)
    own = pl.ds(at, out_ref.shape[0])
    new, new_mean_ref[...], new_square_ref[...] = adam_move(
        col_ref[own, :], total / rows_total, mean_ref[own, :], square_ref[own, :], START + 1
    )
    new_ref[...] = new
    out_ref[...] = col_partial(twice_ref, turned_ref, new, mat_ref, at)


def last_kernel(at, rows_total, count, token_ref, outer_ref, pair_ref, mat_ref, *refs):
    del token_ref
    out_ref, grad_ref, news = refs[-1], refs[5 * count : -1 - count], []
    for index in range(count):
        far_ref, near_ref, col_ref, mean_ref, square_ref = refs[5 * index : 5 * index + 5]
        gradient = pick(outer_ref, far_ref, near_ref) / rows_total
        new, _, _ = adam_move(col_ref[...], gradient, mean_ref[...], square_ref[...], START + 2)
        refs[index - 1 - count][...] = new
        news.append(new)
    high, low = split(jnp.concatenate(news, axis=0))
    twice = jnp.concatenate([high, high], axis=1)
    pair = jnp.concatenate([high, low], axis=1)
    width, rank = high.shape
    for at_row in range(0, mat_ref.shape[0], ROW_BLOCK):
        rows = pl.ds(at_row, ROW_BLOCK)
        slopes = slopes_of(pair_ref[rows, :], twice, mat_ref[rows, pl.ds(at, width)])
        term = jnp.dot(slopes, pair, preferred_element_type=F32)
        term = term[:, :rank] + term[:, rank:]
        out_ref[rows, :] = grad_ref[0][rows, :] + term if grad_ref else term


def store_kernel(token_ref, *refs):
    del token_ref
    *chunk_refs, out_hbm, done_ref, sems = refs
    done_ref[...] = jnp.zeros_like(done_ref)
    stores, at = [], 0
    for index, chunk_ref in enumerate(chunk_refs):
        target = out_hbm.at[pl.ds(at, chunk_ref.shape[0]), :]
        stores.append(pltpu.make_async_copy(chunk_ref, target, sems.at[index]))
        at += chunk_ref.shape[0]
    for store in stores:
        store.start()
    for store in stores:
        store.wait()


def half_share(start, at, width, pair_ref, new, mat_ref, grad_ref, out_refs):
    high, low = split(new)
    twice = jnp.concatenate([high, high], axis=1)
    pair = jnp.concatenate([high, low], axis=1)
    rank, piece = new.shape[1], out_refs[0].shape[0]
    half = piece * len(out_refs)
    rows = pl.ds(pl.multiple_of(start * half, half), half)
    slopes = slopes_of(pair_ref[rows, :], twice, mat_ref[rows, pl.ds(at, width)])
    term = jnp.dot(slopes, pair, preferred_element_type=F32)
    total = grad_ref[rows, :] + term[:, :rank] + term[:, rank:]
    for index, out_ref in enumerate(out_refs):
        out_ref[...] = total[index * piece : (index + 1) * piece]


def send_kernel(
    at, rows_total, token_ref, outer_ref, high_ref, pair_ref, mat_ref, far_ref, near_ref, col_ref, mean_ref,
    square_ref, grad_ref, new_ref, *out_refs,
):
    del token_ref
    gradient = pick(outer_ref, far_ref, near_ref) / rows_total
    new, _, _ = adam_move(col_ref[...], gradient, mean_ref[...], square_ref[...], START + 2)
    new_ref[...] = new
    half_share(1 - high_ref[0], at, new.shape[0], pair_ref, new, mat_ref, grad_ref, out_refs)


def keep_kernel(at, token_ref, high_ref, pair_ref, mat_ref, new_ref, grad_ref, *out_refs):
    del token_ref
    half_share(high_ref[0], at, new_ref.shape[0], pair_ref, new_ref[...], mat_ref, grad_ref, out_refs)


def row_kernel(index, cols_total, token_ref, high_ref, part_ref, other_ref, row_ref, mean_ref, square_ref, new_ref):
    del token_ref
    piece, half = part_ref.shape[0], row_ref.shape[0] // 2
    own = pl.ds(pl.multiple_of(high_ref[0] * half + index * piece, piece), piece)
    gradient = (part_ref[...] + other_ref[...]) / cols_total
    new_ref[...], _, _ = adam_move(row_ref[own, :], gradient, mean_ref[own, :], square_ref[own, :], START + 1)


def join_kernel(high_ref, *refs):
    *piece_refs, out_hbm, sems = refs
    piece, stores = piece_refs[0].shape[0], []
    half = out_hbm.shape[0] // 2
    for index, piece_ref in enumerate(piece_refs):
        far, place = divmod(index, PIECES)
        start = (high_ref[0] if far == 0 else 1 - high_ref[0]) * half + place * piece
        target = out_hbm.at[pl.ds(pl.multiple_of(start, piece), piece), :]
        stores.append(pltpu.make_async_copy(piece_ref, target, sems.at[index]))
    for store in stores:
        store.start()
    for store in stores:
        store.wait()


VMEM = pl.BlockSpec(memory_space=pltpu.VMEM)
SMEM = pl.BlockSpec(memory_space=pltpu.SMEM)
ANY = pl.BlockSpec(memory_space=pl.ANY)
HBM = pl.BlockSpec(memory_space=pltpu.HBM)


def call(kernel, name, ins, outs, scratch=(), aliases=None):
    return pl.pallas_call(
        kernel,
        out_shape=[jax.ShapeDtypeStruct(shape, kind) for _, shape, kind in outs],
        in_specs=[spec for spec, _ in ins],
        out_specs=[spec for spec, _, _ in outs],
        scratch_shapes=scratch,
        input_output_aliases=aliases or {},
        compiler_params=pltpu.CompilerParams(vmem_limit_bytes=6 << 20),
        cost_estimate=pl.CostEstimate(flops=1, bytes_accessed=1, transcendentals=0),
        name=name,
    )(*[pltpu.with_memory_space_constraint(array, pltpu.HBM) if spec is HBM else array for spec, array in ins])


def chunks_of(columns):
    widths = [TARGET] * (columns // TARGET)
    if columns % TARGET:
        widths.append(columns % TARGET)
    return [(sum(widths[:index]), width) for index, width in enumerate(widths)]


class Work:
    def __init__(self, outer, high, halved, matrix, row_factor, col_factor, col_mean, col_square, rows_total):
        self.outer, self.high, self.rows_total = outer, high, rows_total
        self.matrix, self.row = matrix, row_factor
        self.state = [col_factor, col_mean, col_square]
        self.rank = col_factor.shape[1]
        self.chunks = chunks_of(col_factor.shape[0])
        self.moved = {}
        self.new = {}
        self.grad, self.halved = None, halved

    def chunk(self, index):
        return (VMEM, (self.chunks[index][1], self.rank), F32)

    def first(self):
        rows, rank = self.row.shape
        width = sum(self.chunks[1])
        wide = (VMEM, (rows, 2 * rank), BF16)
        self.twice, self.pair, self.turned, out, self.early = call(
            first_kernel, "first",
            [(SMEM, self.outer), (SMEM, self.high), (HBM, self.row), (HBM, self.state[0]), (HBM, self.matrix)],
            [wide, wide, (VMEM, (2 * rank, rows), BF16), self.chunk(0), self.chunk(1)],
            scratch=[
                pltpu.VMEM(self.row.shape, F32),
                pltpu.VMEM((width, rank), F32),
                pltpu.VMEM((rows, width), BF16),
                pltpu.SemaphoreType.DMA((3,)),
            ],
        )
        return out

    def third(self, token):
        col = self.state[0]
        self.state[0], self.matrix, out = call(
            functools.partial(third_kernel, self.chunks[2][0]), "third",
            [(ANY, token), (HBM, col), (HBM, self.matrix), (VMEM, self.twice), (VMEM, self.turned)],
            [(VMEM, col.shape, F32), (VMEM, self.matrix.shape, BF16), self.chunk(2)],
            scratch=[pltpu.SemaphoreType.DMA((3,))],
        )
        return out

    def fresh(self, index, token):
        if index == 1:
            return self.early
        if index == 2:
            return self.third(token)
        (out,) = call(
            functools.partial(fresh_kernel, self.chunks[index][0]), "fresh",
            [(ANY, token), (VMEM, self.twice), (VMEM, self.turned), (VMEM, self.state[0]), (VMEM, self.matrix)],
            [self.chunk(index)],
        )
        return out

    def middle(self, index, far, near, token):
        *self.moved[index], out = call(
            functools.partial(middle_kernel, self.chunks[index][0], self.rows_total), "middle",
            [(ANY, token), (SMEM, self.outer), (VMEM, far), (VMEM, near), (VMEM, self.twice), (VMEM, self.turned)]
            + [(VMEM, array) for array in (self.matrix, *self.state)],
            [self.chunk(index)] * 4,
        )
        return out

    def last(self, indices, far, near, token):
        final = len(self.chunks) - 1
        if self.halved and final in indices:
            if len(indices) > 1:
                self.last(indices[:-1], far, near, token)
                token = self.grad
            return self.halves(final, far[final], near[final], token)
        ins = [(ANY, token), (SMEM, self.outer), (VMEM, self.pair), (VMEM, self.matrix)]
        for index in indices:
            ins += [(VMEM, array) for array in (far[index], near[index], *self.moved[index])]
        aliases = None
        if self.grad is not None:
            aliases = {len(ins): len(indices)}
            ins.append((VMEM, self.grad))
        *new, self.grad = call(
            functools.partial(last_kernel, self.chunks[indices[0]][0], self.rows_total, len(indices)), "last",
            ins,
            [*map(self.chunk, indices), (VMEM, self.row.shape, F32)],
            aliases=aliases,
        )
        self.new.update(zip(indices, new, strict=True))

    def halves(self, index, far, near, token):
        at = self.chunks[index][0]
        rows, rank = self.row.shape
        pieces = [(VMEM, (rows // 2 // PIECES, rank), F32)] * PIECES
        ins = [(VMEM, array) for array in (far, near, *self.moved[index], self.grad)]
        self.new[index], *send = call(
            functools.partial(send_kernel, at, self.rows_total), "send",
            [(ANY, token), (SMEM, self.outer), (SMEM, self.high), (VMEM, self.pair), (VMEM, self.matrix), *ins],
            [self.chunk(index), *pieces],
        )
        keep = call(
            functools.partial(keep_kernel, at), "keep",
            [(ANY, send[0]), (SMEM, self.high)]
            + [(VMEM, array) for array in (self.pair, self.matrix, self.new[index], self.grad)],
            pieces,
        )
        self.ends = keep, send

    def new_cols(self, token):
        return call(
            store_kernel, "store",
            [(ANY, token)] + [(VMEM, self.new[index]) for index in range(len(self.chunks))],
            [(HBM, self.state[0].shape, F32), (VMEM, (8, self.rank), F32)],
            scratch=[pltpu.SemaphoreType.DMA((len(self.chunks),))],
        )


def plain_columns(work):
    every = range(len(work.chunks))
    sums = [lax.psum(work.first(), "row")]
    for index in every[1:]:
        sums.append(lax.psum(work.fresh(index, sums[0]), "row"))
    sums = [lax.psum(work.middle(index, sums[index], sums[index], sums[index]), "row") for index in every]
    for index in every:
        work.last([index], sums, sums, sums[index])


def join_sums_kernel(token_ref, own_ref, arrived_ref, out_ref):
    del token_ref
    out_ref[...] = own_ref[...] + arrived_ref[: out_ref.shape[0], :]


def merge_kernel(which, outer_ref, token_ref, *refs):
    del token_ref
    refs = dict(zip(which, refs, strict=True))
    outer = outer_ref[0] == 1
    if "whole" in refs:
        whole = refs["joined"][...] + refs["from_inner"][...]
        refs["whole"][...] = whole
        if "payload" in refs:
            own = refs["own"][...]
            low, high = sorted((own.shape[0], whole.shape[0]))
            refs["payload"][:low, :] = jnp.where(outer, own[:low], whole[:low])
            if high > low:
                refs["payload"][low:, :] = own[low:] if own.shape[0] == high else whole[low:]
    elif "payload" in refs:
        refs["payload"][...] = refs["own"][...]


def line_columns(work):
    n_col = lax.axis_size("col")
    outer_pairs = [(0, 1), (1, 0), (2, 3), (3, 2)]
    inner_pairs = []
    for col in range(n_col):
        inner_pairs += [(n_col + col, 2 * n_col + col), (2 * n_col + col, n_col + col)]
        inner_pairs += [(at * n_col + col, at * n_col + (col ^ 1)) for at in (0, 3)]
    chunks = len(work.chunks)
    slots = 2 * chunks
    own, joined, whole, from_outer, from_inner = {}, {}, {}, {}, {}
    far, near, pending = {}, {}, []
    own[0] = work.first()
    token = own[0]
    for k in range(slots + 2 * OUTER_LAG + INNER_LAG):
        here = k - OUTER_LAG
        then = here - INNER_LAG
        done = then - OUTER_LAG
        if 0 <= here < slots:
            (joined[here],) = call(
                join_sums_kernel, "sum",
                [(ANY, token), (VMEM, own[here]), (VMEM, from_outer[here])],
                [work.chunk(here % chunks)],
            )
            token = joined[here]
            from_inner[k] = lax.ppermute(joined[here], ("row", "col"), inner_pairs)
        ins, outs = {}, {}
        if 0 <= then < slots:
            ins["joined"], ins["from_inner"] = joined[then], from_inner[k - INNER_LAG]
            outs["whole"] = work.chunk(then % chunks)
            if k < slots:
                ins["own"] = own[k]
                outs["payload"] = max(work.chunk(then % chunks), work.chunk(k % chunks), key=lambda o: o[1])
        if k < OUTER_LAG + INNER_LAG:
            ins["own"], outs["payload"] = own[k], work.chunk(k)
        if outs:
            got = call(
                functools.partial(merge_kernel, [*ins, *outs]), "merge",
                [(SMEM, work.outer), (ANY, token)] + [(VMEM, array) for array in ins.values()],
                [*outs.values()],
            )
            got = dict(zip(outs, got, strict=True))
            token = got[[*outs][-1]]
            if "whole" in got:
                whole[then] = got["whole"]
        if k < slots + OUTER_LAG + INNER_LAG:
            payload = got["payload"] if k < slots else whole[then]
            from_outer[k] = lax.ppermute(payload, "row", outer_pairs)
        early = k - 2 * OUTER_LAG - INNER_LAG + 1
        if k >= slots + INNER_LAG and early < slots:
            at = early - chunks
            (token,) = call(
                pick_kernel, "pick",
                [(SMEM, work.outer), (ANY, token), (VMEM, from_outer[k - OUTER_LAG + 1]), (VMEM, whole[early])],
                [work.chunk(at)],
            )
            far[at] = near[at] = token
            pending.append(at)
        nxt = k + 1
        if nxt < chunks:
            token = own[nxt] = work.fresh(nxt, token)
        elif nxt < slots:
            at = nxt - chunks
            token = own[nxt] = work.middle(at, from_outer[at + OUTER_LAG + INNER_LAG], whole[at], token)
        at = done - chunks
        if at >= 0 and at not in far:
            far[at], near[at] = from_outer[done + OUTER_LAG + INNER_LAG], whole[done]
            pending.append(at)
        pending.sort()
        if pending and nxt >= slots:
            count = BATCH if done + 1 < slots else len(pending)
            batch, pending = pending[:count], pending[count:]
            work.last(batch, far, near, token)
            token = work.grad


def row_step(work, row_mean, row_square, cols_total):
    high = work.high
    rows, rank = work.row.shape
    small = (VMEM, (rows // 2 // PIECES, rank), F32)
    swap = [(0, 1), (1, 0), (2, 3), (3, 2)]
    across = [(0, 2), (2, 0), (1, 3), (3, 1)]
    keep, send = work.ends
    parts = [kept + lax.ppermute(sent, "col", swap) for kept, sent in zip(keep, send, strict=True)]
    others = [lax.ppermute(part, "col", across) for part in parts]
    new_cols, token = work.new_cols(parts[-1])
    news = []
    for index in range(PIECES):
        arrays = (parts[index], others[index], work.row, row_mean, row_square)
        (new,) = call(
            functools.partial(row_kernel, index, cols_total), "row",
            [(ANY, token), (SMEM, high)] + [(VMEM, array) for array in arrays],
            [small],
        )
        news.append(new)
        token = new
    swapped = [lax.ppermute(new, "col", swap) for new in news]
    (out,) = call(
        join_kernel, "join",
        [(SMEM, high)] + [(VMEM, array) for array in (*news, *swapped)],
        [(HBM, work.row.shape, F32)],
        scratch=[pltpu.SemaphoreType.DMA((2 * PIECES,))],
    )
    return out, new_cols


def on_device(matrix, row_factor, col_factor, row_mean, row_square, col_mean, col_square):
    n_row = lax.axis_size("row")
    n_col = lax.axis_size("col")
    row, col = lax.axis_index("row"), lax.axis_index("col")
    outer = ((row == 0) | (row == n_row - 1)).astype(jnp.int32).reshape(1)
    high = (col & 1).astype(jnp.int32).reshape(1)
    work = Work(outer, high, n_col == 4, matrix, row_factor, col_factor, col_mean, col_square, matrix.shape[0] * n_row)
    if n_row == 4 and n_col % 2 == 0:
        line_columns(work)
    else:
        plain_columns(work)
    cols_total = matrix.shape[1] * n_col
    if n_col == 4:
        new_rows, new_cols = row_step(work, row_mean, row_square, cols_total)
    else:
        new_cols, _ = work.new_cols(work.grad)
        summed = lax.psum(work.grad, "col")
        new_rows, _, _ = adam_move(row_factor, summed / cols_total, row_mean, row_square, START + 1)
    return new_rows, new_cols


def solution(mesh):
    return jax.shard_map(
        on_device,
        mesh=mesh,
        in_specs=(
            P(("grp", "row"), "col"),
            P(("grp", "row"), None),
            P(("grp", "col"), None),
            P(("grp", "row"), None),
            P(("grp", "row"), None),
            P(("grp", "col"), None),
            P(("grp", "col"), None),
        ),
        out_specs=(P(("grp", "row"), None), P(("grp", "col"), None)),
        check_vma=False,
    )
```

```python
import functools

import jax
import jax.numpy as jnp
from jax import lax
from jax.experimental import pallas as pl
from jax.experimental.pallas import tpu as pltpu
from jax.sharding import PartitionSpec as P

START = 100
DELTA = 1.0
LEARN_RATE = 0.05
BETA_ONE = 0.9
BETA_TWO = 0.999
EPSILON = 1e-08
F32, BF16 = jnp.float32, jnp.bfloat16
NT = (((1,), (1,)), ((), ()))
ROW_BLOCK = 1024
UNIT = 128
TARGET = 256
OUTER_LAG = 3
INNER_LAG = 2
BATCH = 3
PIECES = 4


def adam_move(values, gradient, first_moment, square, counter):
    first_moment = BETA_ONE * first_moment + (1.0 - BETA_ONE) * gradient
    square = BETA_TWO * square + (1.0 - BETA_TWO) * gradient * gradient
    fixed_mean = first_moment / (1.0 - BETA_ONE**counter)
    fixed_square = square / (1.0 - BETA_TWO**counter)
    return (
        values - LEARN_RATE * fixed_mean / (jnp.sqrt(fixed_square) + EPSILON),
        first_moment,
        square,
    )


def split(values):
    high = values.astype(BF16)
    return high, (values - high.astype(F32)).astype(BF16)


def slopes_of(row_pair, col_pair, block):
    fitted = lax.dot_general(row_pair, col_pair, NT, preferred_element_type=F32)
    return jnp.clip(fitted - block.astype(F32), -DELTA, DELTA).astype(BF16)


def col_partial(twice_ref, turned_ref, col, mat_ref, first_col):
    col_pair = jnp.concatenate(split(col), axis=1)
    width, rank = col.shape
    total = None
    for at in range(0, mat_ref.shape[0], ROW_BLOCK):
        rows = pl.ds(at, ROW_BLOCK)
        slopes = slopes_of(twice_ref[rows, :], col_pair, mat_ref[rows, pl.ds(first_col, width)])
        term = jnp.dot(turned_ref[:, rows], slopes, preferred_element_type=F32)
        total = term if total is None else total + term
    return (total[:rank] + total[rank:]).T


def first_kernel(
    outer_ref, high_ref, row_hbm, col_hbm, mat_hbm, twice_ref, pair_ref, turned_ref, one_ref, two_ref,
    row_ref, col_ref, mat_ref, sems,
):
    del outer_ref, high_ref
    width = col_ref.shape[0]
    loads = [
        pltpu.make_async_copy(row_hbm, row_ref, sems.at[0]),
        pltpu.make_async_copy(mat_hbm.at[:, pl.ds(0, width)], mat_ref, sems.at[1]),
        pltpu.make_async_copy(col_hbm.at[pl.ds(0, width), :], col_ref, sems.at[2]),
    ]
    for load in loads:
        load.start()
    loads[0].wait()
    high, low = split(row_ref[...])
    twice_ref[...] = jnp.concatenate([high, high], axis=1)
    pair_ref[...] = jnp.concatenate([high, low], axis=1)
    turned_ref[...] = jnp.concatenate([high.T, low.T], axis=0)
    loads[1].wait()
    loads[2].wait()
    out = col_partial(twice_ref, turned_ref, col_ref[...], mat_ref, 0)
    one_ref[...] = out[: one_ref.shape[0]]
    two_ref[...] = out[one_ref.shape[0] :]


def third_kernel(
    at, token_ref, col_hbm, mat_hbm, twice_ref, turned_ref, col_ref, mat_ref, out_ref, sems
):
    del token_ref
    width, columns = out_ref.shape[0], mat_ref.shape[1]
    soon = at + width
    loads = [
        pltpu.make_async_copy(mat_hbm.at[:, pl.ds(0, soon)], mat_ref.at[:, pl.ds(0, soon)], sems.at[0]),
        pltpu.make_async_copy(col_hbm, col_ref, sems.at[1]),
    ]
    if soon < columns:
        rest = pl.ds(soon, columns - soon)
        loads.append(pltpu.make_async_copy(mat_hbm.at[:, rest], mat_ref.at[:, rest], sems.at[2]))
    for load in loads:
        load.start()
    loads[0].wait()
    loads[1].wait()
    col = col_ref[pl.ds(at, width), :]
    out_ref[...] = col_partial(twice_ref, turned_ref, col, mat_ref, at)
    for load in loads[2:]:
        load.wait()


def pick(outer_ref, far_ref, near_ref):
    near = near_ref[...]
    return jnp.where(outer_ref[0] == 1, far_ref[: near.shape[0], :], near)


def pick_kernel(outer_ref, token_ref, far_ref, near_ref, out_ref):
    del token_ref
    out_ref[...] = pick(outer_ref, far_ref, near_ref)


def fresh_kernel(at, token_ref, twice_ref, turned_ref, col_ref, mat_ref, out_ref):
    del token_ref
    width = out_ref.shape[0]
    col = col_ref[pl.ds(at, width), :]
    out_ref[...] = col_partial(twice_ref, turned_ref, col, mat_ref, at)


def middle_kernel(
    at, rows_total, token_ref, outer_ref, far_ref, near_ref, twice_ref, turned_ref, mat_ref, col_ref, mean_ref,
    square_ref, new_ref, new_mean_ref, new_square_ref, out_ref,
):
    del token_ref
    total = pick(outer_ref, far_ref, near_ref)
    own = pl.ds(at, out_ref.shape[0])
    new, new_mean_ref[...], new_square_ref[...] = adam_move(
        col_ref[own, :], total / rows_total, mean_ref[own, :], square_ref[own, :], START + 1
    )
    new_ref[...] = new
    out_ref[...] = col_partial(twice_ref, turned_ref, new, mat_ref, at)


def last_kernel(at, rows_total, count, token_ref, outer_ref, pair_ref, mat_ref, *refs):
    del token_ref
    out_ref, grad_ref, news = refs[-1], refs[5 * count : -1 - count], []
    for index in range(count):
        far_ref, near_ref, col_ref, mean_ref, square_ref = refs[5 * index : 5 * index + 5]
        gradient = pick(outer_ref, far_ref, near_ref) / rows_total
        new, _, _ = adam_move(col_ref[...], gradient, mean_ref[...], square_ref[...], START + 2)
        refs[index - 1 - count][...] = new
        news.append(new)
    high, low = split(jnp.concatenate(news, axis=0))
    twice = jnp.concatenate([high, high], axis=1)
    pair = jnp.concatenate([high, low], axis=1)
    width, rank = high.shape
    for at_row in range(0, mat_ref.shape[0], ROW_BLOCK):
        rows = pl.ds(at_row, ROW_BLOCK)
        slopes = slopes_of(pair_ref[rows, :], twice, mat_ref[rows, pl.ds(at, width)])
        term = jnp.dot(slopes, pair, preferred_element_type=F32)
        term = term[:, :rank] + term[:, rank:]
        out_ref[rows, :] = grad_ref[0][rows, :] + term if grad_ref else term


def store_kernel(token_ref, *refs):
    del token_ref
    *chunk_refs, out_hbm, done_ref, sems = refs
    done_ref[...] = jnp.zeros_like(done_ref)
    stores, at = [], 0
    for index, chunk_ref in enumerate(chunk_refs):
        target = out_hbm.at[pl.ds(at, chunk_ref.shape[0]), :]
        stores.append(pltpu.make_async_copy(chunk_ref, target, sems.at[index]))
        at += chunk_ref.shape[0]
    for store in stores:
        store.start()
    for store in stores:
        store.wait()


def half_share(start, at, width, pair_ref, new, mat_ref, grad_ref, out_refs):
    high, low = split(new)
    twice = jnp.concatenate([high, high], axis=1)
    pair = jnp.concatenate([high, low], axis=1)
    rank, piece = new.shape[1], out_refs[0].shape[0]
    half = piece * len(out_refs)
    rows = pl.ds(pl.multiple_of(start * half, half), half)
    slopes = slopes_of(pair_ref[rows, :], twice, mat_ref[rows, pl.ds(at, width)])
    term = jnp.dot(slopes, pair, preferred_element_type=F32)
    total = grad_ref[rows, :] + term[:, :rank] + term[:, rank:]
    for index, out_ref in enumerate(out_refs):
        out_ref[...] = total[index * piece : (index + 1) * piece]


def send_kernel(
    at, rows_total, token_ref, outer_ref, high_ref, pair_ref, mat_ref, far_ref, near_ref, col_ref, mean_ref,
    square_ref, grad_ref, new_ref, *out_refs,
):
    del token_ref
    gradient = pick(outer_ref, far_ref, near_ref) / rows_total
    new, _, _ = adam_move(col_ref[...], gradient, mean_ref[...], square_ref[...], START + 2)
    new_ref[...] = new
    half_share(1 - high_ref[0], at, new.shape[0], pair_ref, new, mat_ref, grad_ref, out_refs)


def keep_kernel(at, token_ref, high_ref, pair_ref, mat_ref, new_ref, grad_ref, *out_refs):
    del token_ref
    half_share(high_ref[0], at, new_ref.shape[0], pair_ref, new_ref[...], mat_ref, grad_ref, out_refs)


def row_kernel(index, cols_total, token_ref, high_ref, part_ref, other_ref, row_ref, mean_ref, square_ref, new_ref):
    del token_ref
    piece, half = part_ref.shape[0], row_ref.shape[0] // 2
    own = pl.ds(pl.multiple_of(high_ref[0] * half + index * piece, piece), piece)
    gradient = (part_ref[...] + other_ref[...]) / cols_total
    new_ref[...], _, _ = adam_move(row_ref[own, :], gradient, mean_ref[own, :], square_ref[own, :], START + 1)


def join_kernel(high_ref, *refs):
    *piece_refs, out_hbm, sems = refs
    piece, stores = piece_refs[0].shape[0], []
    half = out_hbm.shape[0] // 2
    for index, piece_ref in enumerate(piece_refs):
        far, place = divmod(index, PIECES)
        start = (high_ref[0] if far == 0 else 1 - high_ref[0]) * half + place * piece
        target = out_hbm.at[pl.ds(pl.multiple_of(start, piece), piece), :]
        stores.append(pltpu.make_async_copy(piece_ref, target, sems.at[index]))
    for store in stores:
        store.start()
    for store in stores:
        store.wait()


VMEM = pl.BlockSpec(memory_space=pltpu.VMEM)
SMEM = pl.BlockSpec(memory_space=pltpu.SMEM)
ANY = pl.BlockSpec(memory_space=pl.ANY)
HBM = pl.BlockSpec(memory_space=pltpu.HBM)


def call(kernel, name, ins, outs, scratch=(), aliases=None):
    return pl.pallas_call(
        kernel,
        out_shape=[jax.ShapeDtypeStruct(shape, kind) for _, shape, kind in outs],
        in_specs=[spec for spec, _ in ins],
        out_specs=[spec for spec, _, _ in outs],
        scratch_shapes=scratch,
        input_output_aliases=aliases or {},
        compiler_params=pltpu.CompilerParams(vmem_limit_bytes=6 << 20),
        cost_estimate=pl.CostEstimate(flops=1, bytes_accessed=1, transcendentals=0),
        name=name,
    )(*[pltpu.with_memory_space_constraint(array, pltpu.HBM) if spec is HBM else array for spec, array in ins])


def chunks_of(columns):
    widths = [TARGET] * (columns // TARGET)
    if columns % TARGET:
        widths.append(columns % TARGET)
    return [(sum(widths[:index]), width) for index, width in enumerate(widths)]


class Work:
    def __init__(self, outer, high, halved, matrix, row_factor, col_factor, col_mean, col_square, rows_total):
        self.outer, self.high, self.rows_total = outer, high, rows_total
        self.matrix, self.row = matrix, row_factor
        self.state = [col_factor, col_mean, col_square]
        self.rank = col_factor.shape[1]
        self.chunks = chunks_of(col_factor.shape[0])
        self.moved = {}
        self.new = {}
        self.grad, self.halved = None, halved

    def chunk(self, index):
        return (VMEM, (self.chunks[index][1], self.rank), F32)

    def first(self):
        rows, rank = self.row.shape
        width = sum(self.chunks[1])
        wide = (VMEM, (rows, 2 * rank), BF16)
        self.twice, self.pair, self.turned, out, self.early = call(
            first_kernel, "first",
            [(SMEM, self.outer), (SMEM, self.high), (HBM, self.row), (HBM, self.state[0]), (HBM, self.matrix)],
            [wide, wide, (VMEM, (2 * rank, rows), BF16), self.chunk(0), self.chunk(1)],
            scratch=[
                pltpu.VMEM(self.row.shape, F32),
                pltpu.VMEM((width, rank), F32),
                pltpu.VMEM((rows, width), BF16),
                pltpu.SemaphoreType.DMA((3,)),
            ],
        )
        return out

    def third(self, token):
        col = self.state[0]
        self.state[0], self.matrix, out = call(
            functools.partial(third_kernel, self.chunks[2][0]), "third",
            [(ANY, token), (HBM, col), (HBM, self.matrix), (VMEM, self.twice), (VMEM, self.turned)],
            [(VMEM, col.shape, F32), (VMEM, self.matrix.shape, BF16), self.chunk(2)],
            scratch=[pltpu.SemaphoreType.DMA((3,))],
        )
        return out

    def fresh(self, index, token):
        if index == 1:
            return self.early
        if index == 2:
            return self.third(token)
        (out,) = call(
            functools.partial(fresh_kernel, self.chunks[index][0]), "fresh",
            [(ANY, token), (VMEM, self.twice), (VMEM, self.turned), (VMEM, self.state[0]), (VMEM, self.matrix)],
            [self.chunk(index)],
        )
        return out

    def middle(self, index, far, near, token):
        *self.moved[index], out = call(
            functools.partial(middle_kernel, self.chunks[index][0], self.rows_total), "middle",
            [(ANY, token), (SMEM, self.outer), (VMEM, far), (VMEM, near), (VMEM, self.twice), (VMEM, self.turned)]
            + [(VMEM, array) for array in (self.matrix, *self.state)],
            [self.chunk(index)] * 4,
        )
        return out

    def last(self, indices, far, near, token):
        final = len(self.chunks) - 1
        if self.halved and final in indices:
            if len(indices) > 1:
                self.last(indices[:-1], far, near, token)
                token = self.grad
            return self.halves(final, far[final], near[final], token)
        ins = [(ANY, token), (SMEM, self.outer), (VMEM, self.pair), (VMEM, self.matrix)]
        for index in indices:
            ins += [(VMEM, array) for array in (far[index], near[index], *self.moved[index])]
        aliases = None
        if self.grad is not None:
            aliases = {len(ins): len(indices)}
            ins.append((VMEM, self.grad))
        *new, self.grad = call(
            functools.partial(last_kernel, self.chunks[indices[0]][0], self.rows_total, len(indices)), "last",
            ins,
            [*map(self.chunk, indices), (VMEM, self.row.shape, F32)],
            aliases=aliases,
        )
        self.new.update(zip(indices, new, strict=True))

    def halves(self, index, far, near, token):
        at = self.chunks[index][0]
        rows, rank = self.row.shape
        pieces = [(VMEM, (rows // 2 // PIECES, rank), F32)] * PIECES
        ins = [(VMEM, array) for array in (far, near, *self.moved[index], self.grad)]
        self.new[index], *send = call(
            functools.partial(send_kernel, at, self.rows_total), "send",
            [(ANY, token), (SMEM, self.outer), (SMEM, self.high), (VMEM, self.pair), (VMEM, self.matrix), *ins],
            [self.chunk(index), *pieces],
        )
        keep = call(
            functools.partial(keep_kernel, at), "keep",
            [(ANY, send[0]), (SMEM, self.high)]
            + [(VMEM, array) for array in (self.pair, self.matrix, self.new[index], self.grad)],
            pieces,
        )
        self.ends = keep, send

    def new_cols(self, token):
        return call(
            store_kernel, "store",
            [(ANY, token)] + [(VMEM, self.new[index]) for index in range(len(self.chunks))],
            [(HBM, self.state[0].shape, F32), (VMEM, (8, self.rank), F32)],
            scratch=[pltpu.SemaphoreType.DMA((len(self.chunks),))],
        )


def plain_columns(work):
    every = range(len(work.chunks))
    sums = [lax.psum(work.first(), "row")]
    for index in every[1:]:
        sums.append(lax.psum(work.fresh(index, sums[0]), "row"))
    sums = [lax.psum(work.middle(index, sums[index], sums[index], sums[index]), "row") for index in every]
    for index in every:
        work.last([index], sums, sums, sums[index])


def join_sums_kernel(token_ref, own_ref, arrived_ref, out_ref):
    del token_ref
    out_ref[...] = own_ref[...] + arrived_ref[: out_ref.shape[0], :]


def merge_kernel(which, outer_ref, token_ref, *refs):
    del token_ref
    refs = dict(zip(which, refs, strict=True))
    outer = outer_ref[0] == 1
    if "whole" in refs:
        whole = refs["joined"][...] + refs["from_inner"][...]
        refs["whole"][...] = whole
        if "payload" in refs:
            own = refs["own"][...]
            low, high = sorted((own.shape[0], whole.shape[0]))
            refs["payload"][:low, :] = jnp.where(outer, own[:low], whole[:low])
            if high > low:
                refs["payload"][low:, :] = own[low:] if own.shape[0] == high else whole[low:]
    elif "payload" in refs:
        refs["payload"][...] = refs["own"][...]


def line_columns(work):
    n_col = lax.axis_size("col")
    outer_pairs = [(0, 1), (1, 0), (2, 3), (3, 2)]
    inner_pairs = []
    for col in range(n_col):
        inner_pairs += [(n_col + col, 2 * n_col + col), (2 * n_col + col, n_col + col)]
        inner_pairs += [(at * n_col + col, at * n_col + (col ^ 1)) for at in (0, 3)]
    chunks = len(work.chunks)
    slots = 2 * chunks
    own, joined, whole, from_outer, from_inner = {}, {}, {}, {}, {}
    far, near, pending = {}, {}, []
    own[0] = work.first()
    token = own[0]
    for k in range(slots + 2 * OUTER_LAG + INNER_LAG):
        here = k - OUTER_LAG
        then = here - INNER_LAG
        done = then - OUTER_LAG
        if 0 <= here < slots:
            (joined[here],) = call(
                join_sums_kernel, "sum",
                [(ANY, token), (VMEM, own[here]), (VMEM, from_outer[here])],
                [work.chunk(here % chunks)],
            )
            token = joined[here]
            from_inner[k] = lax.ppermute(joined[here], ("row", "col"), inner_pairs)
        ins, outs = {}, {}
        if 0 <= then < slots:
            ins["joined"], ins["from_inner"] = joined[then], from_inner[k - INNER_LAG]
            outs["whole"] = work.chunk(then % chunks)
            if k < slots:
                ins["own"] = own[k]
                outs["payload"] = max(work.chunk(then % chunks), work.chunk(k % chunks), key=lambda o: o[1])
        if k < OUTER_LAG + INNER_LAG:
            ins["own"], outs["payload"] = own[k], work.chunk(k)
        if outs:
            got = call(
                functools.partial(merge_kernel, [*ins, *outs]), "merge",
                [(SMEM, work.outer), (ANY, token)] + [(VMEM, array) for array in ins.values()],
                [*outs.values()],
            )
            got = dict(zip(outs, got, strict=True))
            token = got[[*outs][-1]]
            if "whole" in got:
                whole[then] = got["whole"]
        if k < slots + OUTER_LAG + INNER_LAG:
            payload = got["payload"] if k < slots else whole[then]
            from_outer[k] = lax.ppermute(payload, "row", outer_pairs)
        early = k - 2 * OUTER_LAG - INNER_LAG + 1
        if k >= slots + INNER_LAG and early < slots:
            at = early - chunks
            (token,) = call(
                pick_kernel, "pick",
                [(SMEM, work.outer), (ANY, token), (VMEM, from_outer[k - OUTER_LAG + 1]), (VMEM, whole[early])],
                [work.chunk(at)],
            )
            far[at] = near[at] = token
            pending.append(at)
        nxt = k + 1
        if nxt < chunks:
            token = own[nxt] = work.fresh(nxt, token)
        elif nxt < slots:
            at = nxt - chunks
            token = own[nxt] = work.middle(at, from_outer[at + OUTER_LAG + INNER_LAG], whole[at], token)
        at = done - chunks
        if at >= 0 and at not in far:
            far[at], near[at] = from_outer[done + OUTER_LAG + INNER_LAG], whole[done]
            pending.append(at)
        pending.sort()
        if pending and nxt >= slots:
            count = BATCH if done + 1 < slots else len(pending)
            batch, pending = pending[:count], pending[count:]
            work.last(batch, far, near, token)
            token = work.grad


def row_step(work, row_mean, row_square, cols_total):
    high = work.high
    rows, rank = work.row.shape
    small = (VMEM, (rows // 2 // PIECES, rank), F32)
    swap = [(0, 1), (1, 0), (2, 3), (3, 2)]
    across = [(0, 2), (2, 0), (1, 3), (3, 1)]
    keep, send = work.ends
    parts = [kept + lax.ppermute(sent, "col", swap) for kept, sent in zip(keep, send, strict=True)]
    others = [lax.ppermute(part, "col", across) for part in parts]
    new_cols, token = work.new_cols(parts[-1])
    news = []
    for index in range(PIECES):
        arrays = (parts[index], others[index], work.row, row_mean, row_square)
        (new,) = call(
            functools.partial(row_kernel, index, cols_total), "row",
            [(ANY, token), (SMEM, high)] + [(VMEM, array) for array in arrays],
            [small],
        )
        news.append(new)
        token = new
    swapped = [lax.ppermute(new, "col", swap) for new in news]
    (out,) = call(
        join_kernel, "join",
        [(SMEM, high)] + [(VMEM, array) for array in (*news, *swapped)],
        [(HBM, work.row.shape, F32)],
        scratch=[pltpu.SemaphoreType.DMA((2 * PIECES,))],
    )
    return out, new_cols


def on_device(matrix, row_factor, col_factor, row_mean, row_square, col_mean, col_square):
    n_row = lax.axis_size("row")
    n_col = lax.axis_size("col")
    row, col = lax.axis_index("row"), lax.axis_index("col")
    outer = ((row == 0) | (row == n_row - 1)).astype(jnp.int32).reshape(1)
    high = (col & 1).astype(jnp.int32).reshape(1)
    work = Work(outer, high, n_col == 4, matrix, row_factor, col_factor, col_mean, col_square, matrix.shape[0] * n_row)
    if n_row == 4 and n_col % 2 == 0:
        line_columns(work)
    else:
        plain_columns(work)
    cols_total = matrix.shape[1] * n_col
    if n_col == 4:
        new_rows, new_cols = row_step(work, row_mean, row_square, cols_total)
    else:
        new_cols, _ = work.new_cols(work.grad)
        summed = lax.psum(work.grad, "col")
        new_rows, _, _ = adam_move(row_factor, summed / cols_total, row_mean, row_square, START + 1)
    return new_rows, new_cols


def solution(mesh):
    return jax.shard_map(
        on_device,
        mesh=mesh,
        in_specs=(
            P(("grp", "row"), "col"),
            P(("grp", "row"), None),
            P(("grp", "col"), None),
            P(("grp", "row"), None),
            P(("grp", "row"), None),
            P(("grp", "col"), None),
            P(("grp", "col"), None),
        ),
        out_specs=(P(("grp", "row"), None), P(("grp", "col"), None)),
        check_vma=False,
    )
```
